512 devices in a mesh: gx: 4 (over y), gy: 16 (over z_hi, x, core), gz: 8 (over z_lo).
Axes of the slice: x: 4, y: 4, z: 16 (z_hi: 2, z_lo: 8; z = z_hi * 8 + z_lo), core: 2. Of those that a mesh axis runs over, the one named last changes fastest.
Arguments:
- moving_image: bfloat16 [64, 128, 4096], P('gz', 'gx', 'gy'), may hold values from -6 to 6
- moving_grad: bfloat16 [3, 64, 128, 4096], P(None, 'gz', 'gx', 'gy'), may hold values from -6 to 6
- fixed_grad: bfloat16 [3, 64, 128, 4096], P(None, 'gz', 'gx', 'gy'), may hold values from -6 to 6
- voxel_weight: bfloat16 [64, 128, 4096], P('gz', 'gx', 'gy'), may hold values from 0.01 to 40, as said below
- coefficients: float32 [8, 4, 16, 3, 128], P('gz', 'gx', 'gy'), may hold values from -1 to 1
- weight_table: bfloat16 [8, 256, 128], replicated, may hold values from 0 to 1, as said below
- ctrl_slot: int32 [8, 4, 16, 256, 8], P('gz', 'gx', 'gy'), may hold values from 0 to 26, as said below
- weight_slot: int32 [8, 4, 16, 256, 8], P('gz', 'gx', 'gy'), may hold values from 0 to 7
Outputs:
- new_coefficients: float32 [8, 4, 16, 3, 128], P('gz', 'gx', 'gy')
- warped_image: float32 [64, 128, 4096], P('gz', 'gx', 'gy')
- energies: float32 [2], replicated
The draws below stay inside these ranges and needn't reach their ends.
Inputs may be any that keep to these rules, and one draw needn't show every extreme that they name: `ctrl_slot`: an entry s equals 13 + 9 * dz + 3 * dx + dy, where dz, dx and dy, each -1, 0 or 1, are the offsets of the owning tile along the plane groups, the tile columns and the tile rows, so that s = 13 is the tile itself; for slot k of a block, dz is 0 if bit 2 of k is 0 and else the side of the tile's nearer z face (-1 for the lower half of its planes, +1 for the upper); dx likewise by bit 1 of k and the nearer x face; dy is 0 if bit 0 of k is 0 and else -1 or +1; slot 0 of every block is 13. `voxel_weight`: positive weights. `weight_table`: each entry is a product of cubic B-spline basis values along z, x and y between a voxel of the row and a control point.
All inputs are finite; a program needn't handle non-finite values.
Results may differ from the reference program's by a relative error of at most 0.0003.
Values may be sent and summed in bfloat16 or wider, within the bound.
A program may use at most 64 MiB of HBM per device.

```python
import math
import jax
import jax.numpy as jnp
from jax import lax

TZ = 8
TX = 32
TY = 256
SPACING = 8
NW = 8
K = 8
STEPS = 2
VB = 256
NB = 256
CP = 128
NZ = 64
NX = 128
NY = 4096
N_GX = 4
N_GY = 16
N_GZ = 8


def cubic_basis(offset):
    distance = jnp.abs(offset)
    inner_part = 2.0 / 3.0 - distance * distance + 0.5 * distance ** 3
    outer_part = (2.0 - distance) ** 3 / 6.0
    return jnp.where(distance < 1.0, inner_part, jnp.where(distance < 2.0, outer_part, 0.0))


def draw_voxel_weight(key, part):
    key = jax.random.fold_in(key, 7)
    along_z = jnp.arange(NZ, dtype=jnp.float32)[:, None, None] / NZ
    along_x = jnp.arange(NX, dtype=jnp.float32)[None, :, None] / NX
    along_y = jnp.arange(NY, dtype=jnp.float32)[None, None, :] / NY
    position = along_z + along_x + along_y - 1.5
    rough = jnp.exp(jax.random.uniform(key, (NZ, NX, NY), jnp.float32, math.log(0.3), math.log(3.0)))
    rising = jnp.exp(math.log(3.0) * position)
    return (rising * rough).astype(jnp.bfloat16)


def draw_weight_table(key, part):
    key = jax.random.fold_in(key, 11)
    key_y, key_x, key_z = jax.random.split(key, 3)
    grid_z = TZ // SPACING
    grid_x = TX // SPACING
    grid_y = TY // SPACING
    shift_y = jax.random.uniform(key_y, (NW,), jnp.float32, 0.0, 1.0)
    shift_x = jax.random.uniform(key_x, (NW,), jnp.float32, 0.0, 1.0) * (grid_x - 1)
    shift_z = jax.random.uniform(key_z, (NW,), jnp.float32, 0.0, 1.0) * (grid_z - 1)
    points = jnp.arange(CP, dtype=jnp.int32)
    point_z = (points // (grid_x * grid_y)).astype(jnp.float32)
    point_x = (points // grid_y % grid_x).astype(jnp.float32)
    point_y = (points % grid_y).astype(jnp.float32)
    voxels = (jnp.arange(VB, dtype=jnp.float32) + 0.5) / SPACING
    factor_y = cubic_basis(voxels[None, :, None] - point_y[None, None, :] - shift_y[:, None, None])
    factor_x = cubic_basis(point_x[None, None, :] - shift_x[:, None, None])
    factor_z = cubic_basis(point_z[None, None, :] - shift_z[:, None, None])
    return (factor_y * factor_x * factor_z).astype(jnp.bfloat16)


def draw_ctrl_slot(key, part):
    key = jax.random.fold_in(key, 13)
    blocks = jnp.arange(NB, dtype=jnp.int32)
    plane = blocks // TX
    column = blocks % TX
    side_z = jnp.where(plane < TZ // 2, -1, 1)
    side_x = jnp.where(column < TX // 2, -1, 1)
    coin = jax.random.randint(key, (N_GZ, N_GX, N_GY, NB), 0, 2) * 2 - 1
    side_y = jnp.where(blocks == 0, -1, jnp.where(blocks == NB - 1, 1, coin))
    slots = jnp.arange(K, dtype=jnp.int32)
    bit_z = slots // 4 % 2
    bit_x = slots // 2 % 2
    bit_y = slots % 2
    result = 13 + 9 * bit_z[None, None, None, None, :] * side_z[None, None, None, :, None] + 3 * bit_x[None, None, None, None, :] * side_x[None, None, None, :, None] + bit_y[None, None, None, None, :] * side_y[..., None]
    return result.astype(jnp.int32)


def set_ends(values, rng, smallest, top_value):
    longest = values.shape.index(max(values.shape))
    spots = []
    for shift in (0, 1):
        where = [jax.random.randint(jax.random.fold_in(rng, axis), (), 0, length) for axis, length in enumerate(values.shape)]
        where[longest] = (where[longest] + shift) % values.shape[longest]
        spots.append(tuple(where))
    return values.at[spots[0]].set(smallest).at[spots[1]].set(top_value)


def block_levels(key, dims, cuts, smallest, top_value):
    level, own = 1.0, jax.random.fold_in(key, 6)
    for dim, parts in cuts:
        heights = jnp.exp(jax.random.uniform(jax.random.fold_in(own, dim), (parts,), jnp.float32, smallest / len(cuts), top_value / len(cuts)))
        level = level * jnp.repeat(heights, dims[dim] // parts).reshape([-1 if axis == dim else 1 for axis in range(len(dims))])
    return level


def scatter_about(own_key, extent, scale, reach, cuts=(), kind=jnp.bfloat16):
    loudness = block_levels(own_key, extent, cuts, -0.22, 0.18) if cuts else 1.0
    array = jax.random.normal(own_key, extent, jnp.float32) * scale * loudness
    return jnp.minimum(jnp.maximum(array, -reach), reach).astype(kind)


def setup_inputs(seed: int = 0) -> dict:
    streams_of = jax.random.split(jax.random.key(seed), 9)
    return {
        "moving_image": scatter_about(streams_of[0], (NZ, NX, NY), 1.0, 6.0, ((0, 8), (1, 4), (2, 16))),
        "moving_grad": scatter_about(streams_of[1], (3, NZ, NX, NY), 1.0, 6.0, ((1, 8), (2, 4), (3, 16))),
        "fixed_grad": scatter_about(streams_of[2], (3, NZ, NX, NY), 1.0, 6.0, ((1, 8), (2, 4), (3, 16))),
        "voxel_weight": draw_voxel_weight(jax.random.fold_in(streams_of[8], 71), 0),
        "coefficients": scatter_about(streams_of[4], (N_GZ, N_GX, N_GY, 3, CP), 0.2, 1.0, ((0, 8), (1, 4), (2, 16)), jnp.float32),
        "weight_table": draw_weight_table(jax.random.fold_in(streams_of[8], 71), 0),
        "ctrl_slot": draw_ctrl_slot(jax.random.fold_in(streams_of[8], 71), 0),
        "weight_slot": set_ends(jax.random.randint(streams_of[7], (N_GZ, N_GX, N_GY, NB, K), 0, NW), jax.random.fold_in(streams_of[7], 1), 0, NW - 1).astype(jnp.int32),
    }


EDGE_SQUARED = 0.05
STEP_LENGTH = 0.05
FULL_PRECISION = lax.Precision.HIGHEST

def displacement_field(coefficients, weight_table, ctrl_slot, weight_slot):
    padded = jnp.pad(coefficients, ((1, 1), (1, 1), (1, 1), (0, 0), (0, 0)))
    count_z, count_x, count_y = (coefficients.shape[0], coefficients.shape[1], coefficients.shape[2])
    pieces = []
    for z_offset in range(3):
        for x_offset in range(3):
            for y_offset in range(3):
                pieces.append(padded[z_offset:z_offset + count_z, x_offset:x_offset + count_x, y_offset:y_offset + count_y])
    neighbourhood = jnp.stack(pieces, axis=3)
    table_wide = weight_table.astype(jnp.float32)
    block_products = jnp.einsum('abdsjc,nvc->abdsnjv', neighbourhood, table_wide, precision=FULL_PRECISION)
    block_products = block_products.reshape(count_z, count_x, count_y, 27 * NW, 3 * VB)
    combined = (ctrl_slot * NW + weight_slot).astype(jnp.int32)
    field = jnp.zeros((count_z, count_x, count_y, NB, 3 * VB), jnp.float32)
    for slot_index in range(K):
        field = field + jnp.take_along_axis(block_products, combined[..., slot_index][..., None], axis=3)
    field = field.reshape(count_z, count_x, count_y, TZ, TX, 3, TY)
    field = jnp.transpose(field, (5, 0, 3, 1, 4, 2, 6))
    return field.reshape(3, NZ, NX, NY)

def central_grad(padded):
    along_z = (padded[2:, 1:-1, 1:-1] - padded[:-2, 1:-1, 1:-1]) * 0.5
    along_x = (padded[1:-1, 2:, 1:-1] - padded[1:-1, :-2, 1:-1]) * 0.5
    along_y = (padded[1:-1, 1:-1, 2:] - padded[1:-1, 1:-1, :-2]) * 0.5
    return (along_z, along_x, along_y)

def objective(coefficients, moving_image, moving_grad, fixed_grad, voxel_weight, weight_table, ctrl_slot, weight_slot):
    field = displacement_field(coefficients, weight_table, ctrl_slot, weight_slot)
    moving_wide = moving_grad.astype(jnp.float32)
    warped = moving_image.astype(jnp.float32) + field[0] * moving_wide[0] + field[1] * moving_wide[1] + field[2] * moving_wide[2]
    grads = central_grad(jnp.pad(warped, 1))
    fixed_wide = fixed_grad.astype(jnp.float32)
    inner = grads[0] * fixed_wide[0] + grads[1] * fixed_wide[1] + grads[2] * fixed_wide[2]
    fixed_sq = fixed_wide[0] ** 2 + fixed_wide[1] ** 2 + fixed_wide[2] ** 2 + EDGE_SQUARED
    moving_sq = grads[0] ** 2 + grads[1] ** 2 + grads[2] ** 2 + EDGE_SQUARED
    terms = voxel_weight.astype(jnp.float32) * (1.0 - inner * inner / (fixed_sq * moving_sq))
    return (jnp.sum(terms), warped)

def reference(moving_image, moving_grad, fixed_grad, voxel_weight, coefficients, weight_table, ctrl_slot, weight_slot):
    current = coefficients
    energy_list = []
    warped = None
    for step_index in range(STEPS):
        (total, warped), gradient = jax.value_and_grad(objective, has_aux=True)(current, moving_image, moving_grad, fixed_grad, voxel_weight, weight_table, ctrl_slot, weight_slot)
        energy_list.append(total / float(NZ * NX * NY))
        step_size = STEP_LENGTH / jnp.sqrt(jnp.mean(gradient * gradient) + 1e-06)
        current = current - step_size * gradient
    return (current, warped, jnp.stack(energy_list))
```

```python
import functools

import jax
import jax.numpy as jnp
from jax import lax
from jax.experimental import pallas as pl
from jax.experimental.pallas import tpu as pltpu
from jax.sharding import PartitionSpec as P

MESH = pl.DeviceIdType.MESH
F32 = jnp.float32
BF16 = jnp.bfloat16
EDGE_SQUARED = 0.05
STEP_LENGTH = 0.05
NX, NY, NZ = 4, 16, 8
TZ, TX, TY, CP, NW = 8, 32, 256, 128, 8
ROWS = TZ * TX
REACH = 45
FIRST = 7
CENTRE = FIRST + 22
MAIN = FIRST + 9
HALO = 80


def split(x):
    high = x.astype(BF16)
    return high, (x - high.astype(F32)).astype(BF16)


def stacked(x):
    return jnp.concatenate(split(x), axis=0)


def dot(a, b):
    return jnp.dot(a, b, preferred_element_type=F32)


def dot_nt(a, b):
    return lax.dot_general(a, b, (((1,), (1,)), ((), ())), preferred_element_type=F32)


def iota(shape, dim):
    return lax.broadcasted_iota(jnp.int32, shape, dim)


def offset_of(i):
    group = i // 9
    rest = i - group * 9
    dy = (2 - group // 2) * (2 * (group % 2) - 1)
    dz = rest // 3 - 1
    dx = rest % 3 - 1
    return dz, dx, dy


def kernel(
    mi, mg, fg, vw, co, tb, cs, ws,
    out_c, out_w, out_e,
    NB, PB, RB, AP, AZ, CB, CBH, HZ, HX, XS, XC, YS, YR, P2, PT2, PY2, PYT2, MGS, YC, BHL,
    WP, WX, WY, IFS, FZ, PU, PUX, PYB, WG, GS, TF, TE, YT,
    nb_send, nb_recv, rb_send, rb_recv, face_send, face_recv, ap_send, ap_recv, az_send, az_recv,
):
    gx, gy, gz = lax.axis_index("gx"), lax.axis_index("gy"), lax.axis_index("gz")
    lane = iota((1, 128), 1)
    plane_at = gx * 8 + gy % 8
    ring_at = (gy // 8) * 8 + gz

    def plane_peer(r):
        other = (plane_at + r) % 32
        return (other // 8, (gy // 8) * 8 + other % 8, gz)

    def ring_peer(r):
        other = (ring_at + r) % 16
        return (gx, (other // 8) * 8 + gy % 8, other % 8)

    def neighbour(i):
        dz, dx, dy = offset_of(i)
        z, x, y = gz + dz, gx + dx, gy + dy
        there = (z >= 0) & (z < NZ) & (x >= 0) & (x < NX) & (y >= 0) & (y < NY) & (i != 40)
        u = (dy + 2) * 9 + (dz + 1) * 3 + dx + 1
        return there, (x, y, z), u

    def each(count, body, start=0):
        def step(i, carry):
            body(i)
            return carry

        lax.fori_loop(start, count, step, 0)

    for ref in (NB, RB, CB, CBH, HZ, HX, YR):
        ref[...] = jnp.zeros(ref.shape, ref.dtype)
    for c in range(3):
        NB[0, c, CENTRE : CENTRE + 1, :] = co[c : c + 1, :]

    barrier = pltpu.get_barrier_semaphore()

    def greet(i):
        there, where, _ = neighbour(i)

        @pl.when(there)
        def _():
            pl.semaphore_signal(barrier, inc=1, device_id=where, device_id_type=MESH)

    each(REACH, greet)

    def greet_plane(r):
        pl.semaphore_signal(barrier, inc=1, device_id=plane_peer(r), device_id_type=MESH)

    def greet_ring(r):
        pl.semaphore_signal(barrier, inc=1, device_id=ring_peer(r), device_id_type=MESH)

    each(16, greet_ring, 1)
    each(32, greet_plane, 1)

    slot = cs[...]
    third = (slot * 11) >> 5
    comb = ws[...] * 32 + (slot - 3 * third) * 9 + third
    CB[:, 0:8] = comb.astype(F32)
    four = [mi] + [mg.at[c] for c in range(3)]
    wide = [ref[...].astype(F32).reshape(ROWS, TY) for ref in four]
    for c in range(3):
        MGS[c, 0:ROWS, :] = wide[1 + c]
    for f, column in ((0, TY - 1), (1, 0)):
        packed = CB[...]
        for a in range(4):
            packed = jnp.where(lane == 8 + a, wide[a][:, column : column + 1], packed)
        YS[f] = packed.T[0:16, :]
    for f, row in ((0, TX - 1), (1, 0)):
        for z in range(TZ):
            m = z * TX + row
            for a in range(4):
                XS[f, a * 8 + z : a * 8 + z + 1, :] = wide[a][m : m + 1, :]
            XC[f, z : z + 1, :] = CB[m : m + 1, :]

    count_z = 3 - (gz == 0).astype(jnp.int32) - (gz == NZ - 1).astype(jnp.int32)
    count_x = 3 - (gx == 0).astype(jnp.int32) - (gx == NX - 1).astype(jnp.int32)
    count_y = jnp.minimum(gy, 2) + jnp.minimum(NY - 1 - gy, 2) + 1
    pl.semaphore_wait(barrier, count_z * count_x * count_y - 1 + 46)

    def block_copy(buffer_from, row_from, buffer_to, row_to, send, recv, where):
        return pltpu.make_async_remote_copy(
            src_ref=buffer_from.at[:, pl.ds(row_from, 1), :],
            dst_ref=buffer_to.at[:, pl.ds(row_to, 1), :],
            send_sem=send, recv_sem=recv, device_id=where, device_id_type=MESH,
        )

    def spread_copy(k, i):
        there, where, u = neighbour(i)
        return there, block_copy(
            NB.at[k], CENTRE, NB.at[k], FIRST + 44 - u, nb_send.at[k, u], nb_recv.at[k, 44 - u], where
        )

    def gather_copy(k, i):
        there, where, u = neighbour(i)
        return there, block_copy(
            PB.at[k], FIRST + u, RB.at[k], FIRST + 44 - u, rb_send.at[k, u], rb_recv.at[k, 44 - u], where
        )

    def start(maker, k):
        def body(i):
            there, copy = maker(k, i)
            pl.when(there)(copy.start)

        each(REACH, body)

    def finish_send(maker, k):
        def body(i):
            there, copy = maker(k, i)
            pl.when(there)(copy.wait_send)

        each(REACH, body)

    def finish_recv(buffer, recv, k):
        def body(i):
            there, where, u = neighbour(i)
            copy = block_copy(buffer.at[k], FIRST + u, buffer.at[k], FIRST + u, recv.at[k, u], recv.at[k, u], where)
            pl.when(there)(copy.wait_recv)

        each(REACH, body)

    def face_copies():
        result = []

        def add(n, src, dst, where, sends, gets):
            copy = pltpu.make_async_remote_copy(
                src_ref=src, dst_ref=dst, send_sem=face_send.at[n], recv_sem=face_recv.at[n],
                device_id=where, device_id_type=MESH,
            )
            result.append((copy, sends, gets))

        for f, side in ((0, 1), (1, -1)):
            ahead = (gy < NY - 1) if f == 0 else (gy > 0)
            behind = (gy > 0) if f == 0 else (gy < NY - 1)
            add(f, YS.at[f], YR.at[f], (gx, gy + side, gz), ahead, behind)
        for f, side in ((0, 1), (1, -1)):
            ahead = (gz < NZ - 1) if f == 0 else (gz > 0)
            behind = (gz > 0) if f == 0 else (gz < NZ - 1)
            at = TZ - 1 if f == 0 else 0
            where = (gx, gy, gz + side)
            add(2 + f, mi.at[at], HZ.at[f, 0], where, ahead, behind)
            add(4 + f, mg.at[:, at], HZ.at[f, pl.ds(1, 3)], where, ahead, behind)
            add(6 + f, CB.at[pl.ds(at * TX, TX)], CBH.at[pl.ds(f * TX, TX)], where, ahead, behind)
        for f, side in ((0, 1), (1, -1)):
            ahead = (gx < NX - 1) if f == 0 else (gx > 0)
            behind = (gx > 0) if f == 0 else (gx < NX - 1)
            where = (gx + side, gy, gz)
            add(8 + f, XS.at[f], HX.at[f], where, ahead, behind)
            add(10 + f, XC.at[f], CBH.at[pl.ds(64 + f * 8, 8)], where, ahead, behind)
        return result

    def sum_copy(buffer, k, at, where, send, recv):
        return pltpu.make_async_remote_copy(
            src_ref=buffer.at[k, pl.ds(at, 1)], dst_ref=buffer.at[k, pl.ds(at, 1)],
            send_sem=send.at[k], recv_sem=recv.at[k], device_id=where, device_id_type=MESH,
        )

    def sum_all(buffer, k, count, send, recv):
        return pltpu.make_async_remote_copy(
            src_ref=buffer.at[k, pl.ds(0, count)], dst_ref=buffer.at[k, pl.ds(0, count)],
            send_sem=send.at[k], recv_sem=recv.at[k], device_id=plane_peer(1), device_id_type=MESH,
        )

    faces = face_copies()
    for copy, sends, _ in faces[:2]:
        pl.when(sends)(copy.start)
    start(spread_copy, 0)
    for copy, sends, _ in faces[2:]:
        pl.when(sends)(copy.start)

    which = iota((256, 256), 0).astype(F32)

    def picked(rows):
        hit = jnp.zeros((256, rows.shape[1]), F32)
        for k in range(8):
            hit = hit + jnp.where(rows[k : k + 1, :] == which[:, 0 : rows.shape[1]], 1.0, 0.0)
        return hit

    own = picked(CB[...].T[0:8, :])
    PT2[:, 0:256] = own.astype(BF16)
    PT2[:, 384:640] = own.astype(BF16)
    own_t = own.T.astype(BF16)
    P2[0:256, 0:256] = own_t
    P2[0:256, 256:512] = own_t
    for c in range(3):
        for n in range(NW):
            TF[c * 16 + n : c * 16 + n + 1, :] = tb[n, TY - 16 : TY, :].astype(F32)[15:16, :]
            TF[c * 16 + 8 + n : c * 16 + 9 + n, :] = tb[n, 0:16, :].astype(F32)[0:1, :]
    TF[48:128, :] = jnp.zeros((80, CP), F32)
    TE[...] = TF[...].astype(BF16)
    fixed = [fg[c].astype(F32) for c in range(3)]
    IFS[...] = 1.0 / (fixed[0] * fixed[0] + fixed[1] * fixed[1] + fixed[2] * fixed[2] + EDGE_SQUARED)
    WG[...] = jnp.zeros(WG.shape, BF16)
    for at in (0, 1, 10, 11):
        FZ[at] = jnp.zeros((TX, TY), F32)
    PB[...] = jnp.zeros(PB.shape, F32)

    for copy, _, gets in faces:
        pl.when(gets)(copy.wait_recv)
    finish_recv(NB, nb_recv, 0)

    column = iota((1, 128), 1)
    shift = jnp.where(column < 32, -3.0, jnp.where(column < 64, 3.0, jnp.where(column < 72, -1.0, 1.0)))
    halo = picked(CBH[...].T[0:8, :] + shift)
    PT2[:, 256:384] = halo.astype(BF16)
    PT2[:, 640:768] = halo.astype(BF16)
    halo_t = halo.T.astype(BF16)
    P2[256:384, 0:256] = halo_t
    P2[256:384, 256:512] = halo_t
    for c in range(3):
        MGS[c, 256:288, :] = HZ[0, 1 + c].astype(F32)
        MGS[c, 288:320, :] = HZ[1, 1 + c].astype(F32)
        MGS[c, 320:328, :] = HX[0, 8 + c * 8 : 16 + c * 8, :]
        MGS[c, 328:336, :] = HX[1, 8 + c * 8 : 16 + c * 8, :]
    YT[...] = jnp.zeros((128, 256), F32)
    for f in range(2):
        for c in range(3):
            YT[c * 16 : c * 16 + 16, :] = jnp.broadcast_to(YR[f, 9 + c : 10 + c, :], (16, 256))
        YT[48:49, :] = YR[f, 8:9, :]
        YC[f] = YT[...].T
        side = picked(YR[f, 0:8, :])
        PYT2[f, :, 0:256] = side.astype(BF16)
        PYT2[f, :, 256:512] = side.astype(BF16)
        side_t = side.T.astype(BF16)
        PY2[f, :, 0:256] = side_t
        PY2[f, :, 256:512] = side_t

    def forward(k):
        near = stacked(jnp.concatenate([NB[k, c, MAIN : MAIN + 32, :] for c in range(3)], axis=0))
        for n in range(NW):
            product = dot_nt(near, tb[n])
            high, low = split(product[0:96] + product[96:192])
            for c in range(3):
                BHL[c, n * 32 : n * 32 + 32, :] = high[c * 32 : c * 32 + 32]
                BHL[c, 256 + n * 32 : 288 + n * 32, :] = low[c * 32 : c * 32 + 32]
        total = None
        for c in range(3):
            part = dot(P2[0:336, :], BHL[c]) * MGS[c]
            total = part if total is None else total + part
        wide_blocks = stacked(jnp.concatenate([NB[k, c] for c in range(3)], axis=0))
        ends = dot_nt(wide_blocks, TE[...])
        ends = ends[0:192] + ends[192:384]
        columns = []
        for f in range(2):
            at = FIRST + 18 * f
            chosen = jnp.zeros((32, 128), F32)
            for c in range(3):
                chosen = jnp.where(lane // 16 == c, ends[c * 64 + at : c * 64 + at + 32], chosen)
            spread = jnp.concatenate(
                [jnp.where(lane % 16 == n + 8 * f, chosen, 0.0) for n in range(NW)], axis=0
            )
            columns.append(jnp.sum(dot(PY2[f], stacked(spread)) * YC[f], axis=1, keepdims=True))
        return total, columns

    total, columns = forward(0)
    WP[1:9] = mi[...].astype(F32) + total[0:256].reshape(TZ, TX, TY)
    for f, at in ((0, 0), (1, 9)):
        WP[at] = HZ[f, 0].astype(F32) + total[256 + 32 * f : 288 + 32 * f]
        WX[f] = HX[f, 0:8, :] + total[320 + 8 * f : 328 + 8 * f]
        WY[f] = jnp.broadcast_to(YC[f, :, 48:49] + columns[f], (256, 128))

    row_at = iota((TX, TY), 0)
    lane_at = iota((TX, TY), 1)

    def backward(k):
        def plane(z, energy):
            here = WP[z + 1]
            rows = pl.ds(pl.multiple_of(z * TX, TX), TX)
            back_x, on_x = pltpu.roll(here, 1, 0), pltpu.roll(here, TX - 1, 0)
            back_x = jnp.where(row_at == 0, WX[0, pl.ds(z, 1), :], back_x)
            on_x = jnp.where(row_at == TX - 1, WX[1, pl.ds(z, 1), :], on_x)
            back_y, on_y = pltpu.roll(here, 1, 1), pltpu.roll(here, TY - 1, 1)
            side = WY[0, rows, :]
            back_y = jnp.where(lane_at == 0, jnp.concatenate([side, side], axis=1), back_y)
            side = WY[1, rows, :]
            on_y = jnp.where(lane_at == TY - 1, jnp.concatenate([side, side], axis=1), on_y)
            grads = (WP[z + 2] - WP[z], on_x - back_x, on_y - back_y)
            fixed = [fg[c, z].astype(F32) for c in range(3)]
            inner = (grads[0] * fixed[0] + grads[1] * fixed[1] + grads[2] * fixed[2]) * 0.5
            moving = (grads[0] * grads[0] + grads[1] * grads[1] + grads[2] * grads[2]) * 0.25 + EDGE_SQUARED
            inverse = 1.0 / moving
            weight = vw[z].astype(F32)
            scaled = weight * inner * IFS[z] * inverse
            term = weight - inner * scaled
            other = 0.5 * scaled * inner * inverse
            flux = [other * grads[c] - scaled * fixed[c] for c in range(3)]
            FZ[z + 2] = flux[0]
            pulled = jnp.where(row_at == 0, 0.0, pltpu.roll(flux[1], 1, 0))
            pulled = pulled - jnp.where(row_at == TX - 1, 0.0, pltpu.roll(flux[1], TX - 1, 0))
            pulled = pulled + jnp.where(lane_at == 0, 0.0, pltpu.roll(flux[2], 1, 1))
            pulled = pulled - jnp.where(lane_at == TY - 1, 0.0, pltpu.roll(flux[2], TY - 1, 1))
            PU[z] = pulled
            PUX[0, pl.ds(z, 1), :] = -flux[1][0:1, :]
            PUX[1, pl.ds(z, 1), :] = flux[1][TX - 1 : TX, :]
            PYB[0, rows, :] = jnp.broadcast_to(-flux[2][:, 0:1], (TX, 128))
            PYB[1, rows, :] = jnp.broadcast_to(flux[2][:, TY - 1 : TY], (TX, 128))
            return energy + term

        energy = lax.fori_loop(0, TZ, plane, jnp.zeros((TX, TY), F32))
        energy = jnp.sum(energy, axis=0, keepdims=True)

        def put(block, rows, at):
            for c in range(3):
                high, low = split(block * MGS[c, pl.ds(at, rows), :])
                WG[c, pl.ds(at, rows), :] = high
                WG[c, pl.ds(at + 384, rows), :] = low

        def weigh(z, carry):
            put(PU[z] + FZ[z + 1] - FZ[z + 3], TX, pl.multiple_of(z * TX, TX))
            return carry

        lax.fori_loop(0, TZ, weigh, 0)
        put(-FZ[2], TX, 256)
        put(FZ[9], TX, 288)
        put(jnp.concatenate([PUX[0], PUX[1]], axis=0), 16, 320)
        for c in range(3):
            high, low = split(dot(PT2[...], WG[c]))
            for n in range(NW):
                GS[c * 32 : c * 32 + 32, n * 256 : n * 256 + 256] = high[n * 32 : n * 32 + 32]
                GS[96 + c * 32 : 128 + c * 32, n * 256 : n * 256 + 256] = low[n * 32 : n * 32 + 32]
        partial = dot(GS[...], tb[...].reshape(NW * TY, CP))
        partial = partial[0:96] + partial[96:192]
        for c in range(3):
            PB[k, c, MAIN : MAIN + 32, :] = partial[c * 32 : c * 32 + 32]
        for f in range(2):
            drawn = jnp.where(lane < 48, PYB[f] * YC[f], 0.0)
            back = dot(PYT2[f], stacked(drawn))
            chosen = jnp.zeros((32, 128), F32)
            for n in range(NW):
                chosen = jnp.where(lane % 16 == n + 8 * f, back[n * 32 : n * 32 + 32], chosen)
            blocks = jnp.concatenate([jnp.where(lane // 16 == c, chosen, 0.0) for c in range(3)], axis=0)
            ends = dot(stacked(blocks), TE[...])
            ends = ends[0:96] + ends[96:192]
            at = FIRST + 18 * f
            for c in range(3):
                PB[k, c, at : at + 32, :] = PB[k, c, at : at + 32, :] + ends[c * 32 : c * 32 + 32]
        return energy[:, 0:128] + energy[:, 128:256]

    def reduce_gradient(k, energy):
        start(gather_copy, k)
        for c in range(3):
            RB[k, c, CENTRE : CENTRE + 1, :] = PB[k, c, CENTRE : CENTRE + 1, :]
        finish_recv(RB, rb_recv, k)
        gradient = [jnp.sum(RB[k, c], axis=0, keepdims=True) for c in range(3)]
        square = gradient[0] * gradient[0] + gradient[1] * gradient[1] + gradient[2] * gradient[2]
        energy = energy + pltpu.roll(energy, 64, 1)
        square = square + pltpu.roll(square, 64, 1)
        AP[k, pl.ds(plane_at, 1), :] = jnp.where(lane < 64, energy, square)
        each(32, lambda r: sum_copy(AP, k, plane_at, plane_peer(r), ap_send, ap_recv).start(), 1)
        return gradient

    def pass_on(k):
        sum_all(AP, k, 31, ap_send, ap_recv).wait_recv()
        AZ[k, pl.ds(ring_at, 1), :] = jnp.sum(AP[k], axis=0, keepdims=True)
        each(16, lambda r: sum_copy(AZ, k, ring_at, ring_peer(r), az_send, az_recv).start(), 1)

    def take_sum(k):
        sum_all(AZ, k, 15, az_send, az_recv).wait_recv()
        sums = jnp.sum(AZ[k], axis=0, keepdims=True)
        energy = jnp.sum(jnp.where(lane < 64, sums, 0.0), axis=1, keepdims=True)
        square = jnp.sum(jnp.where(lane < 64, 0.0, sums), axis=1, keepdims=True)
        devices = NX * NY * NZ
        step_size = STEP_LENGTH * lax.rsqrt(square * (1.0 / (devices * 3 * CP)) + 1e-06)
        return energy * (1.0 / (devices * TZ * TX * TY)), step_size

    energy = backward(0)
    first = reduce_gradient(0, energy)
    for c in range(3):
        NB[1, c, CENTRE : CENTRE + 1, :] = first[c]
    start(spread_copy, 1)
    pass_on(0)
    for copy, sends, _ in faces:
        pl.when(sends)(copy.wait_send)
    finish_send(spread_copy, 0)
    finish_recv(NB, nb_recv, 1)
    total, columns = forward(1)
    energy_0, size_0 = take_sum(0)
    WP[1:9] = WP[1:9] - size_0[0, 0] * total[0:256].reshape(TZ, TX, TY)
    for f, at in ((0, 0), (1, 9)):
        WP[at] = WP[at] - size_0 * total[256 + 32 * f : 288 + 32 * f]
        WX[f] = WX[f] - size_0 * total[320 + 8 * f : 328 + 8 * f]
        WY[f] = WY[f] - size_0 * columns[f]
    out_w[...] = WP[1:9]
    energy = backward(1)
    second = reduce_gradient(1, energy)
    finish_send(gather_copy, 0)
    finish_send(spread_copy, 1)
    sum_all(AP, 0, 31, ap_send, ap_recv).wait_send()
    sum_all(AZ, 0, 15, az_send, az_recv).wait_send()
    pass_on(1)
    finish_send(gather_copy, 1)
    sum_all(AP, 1, 31, ap_send, ap_recv).wait_send()
    energy_1, size_1 = take_sum(1)
    sum_all(AZ, 1, 15, az_send, az_recv).wait_send()
    for c in range(3):
        out_c[c : c + 1, :] = co[c : c + 1, :] - size_0 * first[c] - size_1 * second[c]
    out_e[0] = energy_0[0, 0]
    out_e[1] = energy_1[0, 0]


def on_device(moving_image, moving_grad, fixed_grad, voxel_weight, coefficients, weight_table, ctrl_slot, weight_slot):
    whole = pl.BlockSpec(memory_space=pltpu.VMEM)
    vmem = pltpu.VMEM
    sem = pltpu.SemaphoreType.DMA
    new, warped, energies = pl.pallas_call(
        kernel,
        out_shape=(
            jax.ShapeDtypeStruct((3, CP), F32),
            jax.ShapeDtypeStruct((TZ, TX, TY), F32),
            jax.ShapeDtypeStruct((2,), F32),
        ),
        in_specs=[whole] * 8,
        out_specs=(whole, whole, pl.BlockSpec(memory_space=pltpu.SMEM)),
        scratch_shapes=[
            vmem((2, 3, 64, CP), F32),
            vmem((2, 3, 64, CP), F32),
            vmem((2, 3, 64, CP), F32),
            vmem((2, 32, 128), F32),
            vmem((2, 16, 128), F32),
            vmem((256, 128), F32),
            vmem((128, 128), F32),
            vmem((2, 4, TX, TY), BF16),
            vmem((2, 32, TY), F32),
            vmem((2, 32, TY), F32),
            vmem((2, 8, 128), F32),
            vmem((2, 16, TY), F32),
            vmem((2, 16, TY), F32),
            vmem((384, 512), BF16),
            vmem((256, 768), BF16),
            vmem((2, 256, 512), BF16),
            vmem((2, 256, 512), BF16),
            vmem((3, 336, TY), F32),
            vmem((2, 256, 128), F32),
            vmem((3, 512, TY), BF16),
            vmem((10, TX, TY), F32),
            vmem((2, 8, TY), F32),
            vmem((2, 256, 128), F32),
            vmem((TZ, TX, TY), F32),
            vmem((12, TX, TY), F32),
            vmem((TZ, TX, TY), F32),
            vmem((2, 8, TY), F32),
            vmem((2, 256, 128), F32),
            vmem((3, 768, TY), BF16),
            vmem((192, 2048), BF16),
            vmem((128, CP), F32),
            vmem((128, CP), BF16),
            vmem((128, 256), F32),
            sem((2, REACH)), sem((2, REACH)), sem((2, REACH)), sem((2, REACH)),
            sem((12,)), sem((12,)), sem((2,)), sem((2,)), sem((2,)), sem((2,)),
        ],
        compiler_params=pltpu.CompilerParams(
            collective_id=0, has_side_effects=True, vmem_limit_bytes=48 * 1024 * 1024
        ),
    )(
        moving_image, moving_grad, fixed_grad, voxel_weight, coefficients.reshape(3, CP), weight_table,
        ctrl_slot.reshape(ROWS, 8), weight_slot.reshape(ROWS, 8),
    )
    return new.reshape(1, 1, 1, 3, CP), warped, energies


def solution(mesh):
    in_specs = (
        P("gz", "gx", "gy"),
        P(None, "gz", "gx", "gy"),
        P(None, "gz", "gx", "gy"),
        P("gz", "gx", "gy"),
        P("gz", "gx", "gy", None, None),
        P(),
        P("gz", "gx", "gy", None, None),
        P("gz", "gx", "gy", None, None),
    )
    out_specs = (P("gz", "gx", "gy", None, None), P("gz", "gx", "gy"), P())
    return jax.shard_map(on_device, mesh=mesh, in_specs=in_specs, out_specs=out_specs, check_vma=False)
```

```python
import functools

import jax
import jax.numpy as jnp
from jax import lax
from jax.experimental import pallas as pl
from jax.experimental.pallas import tpu as pltpu
from jax.sharding import PartitionSpec as P

MESH = pl.DeviceIdType.MESH
F32 = jnp.float32
BF16 = jnp.bfloat16
EDGE_SQUARED = 0.05
STEP_LENGTH = 0.05
NX, NY, NZ = 4, 16, 8
TZ, TX, TY, CP, NW = 8, 32, 256, 128, 8
ROWS = TZ * TX
FIRST = 7
CENTRE = FIRST + 22
MAIN = FIRST + 9
HALO = 80


def split(x):
    high = x.astype(BF16)
    return high, (x - high.astype(F32)).astype(BF16)


def stacked(x):
    return jnp.concatenate(split(x), axis=0)


def dot(a, b):
    return jnp.dot(a, b, preferred_element_type=F32)


def dot_nt(a, b):
    return lax.dot_general(a, b, (((1,), (1,)), ((), ())), preferred_element_type=F32)


def iota(shape, dim):
    return lax.broadcasted_iota(jnp.int32, shape, dim)


NEAR = [
    (dz, dx, dy) for dy in (2, -2, 1, -1, 0) for dx in (-1, 0, 1) for dz in (-1, 0, 1) if (dz, dx, dy) != (0, 0, 0)
]
COUNTS = sorted({a * b * c - 1 for a in (2, 3) for b in (2, 3) for c in (3, 4, 5)})


def index_of(dz, dx, dy):
    return (dy + 2) * 9 + (dz + 1) * 3 + dx + 1


def kernel(
    mi_in, mg_in, fg_in, vw_in, co_in, tb_in, cs_in, ws_in,
    out_c, out_w, out_e,
    mi, mg, fg, vw, tb, cs, ws,
    NB, PB, RB, AP, AZ, CT, HC, SEL, HZ, HX, XS, YS, YR, P2, PT2, PY2, PYT2, MGS, YC, BHL,
    WP, WX, WY, IFS, FZ, PU, PUX, PYB, WG, GS, TF, TE, YT,
    in_sem, nb_send, nb_recv, rb_send, rb_recv, face_send, face_recv, ap_send, ap_recv, az_send, az_recv,
):
    gx, gy, gz = lax.axis_index("gx"), lax.axis_index("gy"), lax.axis_index("gz")
    lane = iota((1, 128), 1)
    plane_at = gx * 8 + gy % 8
    ring_at = (gy // 8) * 8 + gz

    mine = (gx, gy, gz)

    def plane_peer(r):
        other = (plane_at + r) % 32
        return (other // 8, (gy // 8) * 8 + other % 8, gz)

    def ring_peer(r):
        other = (ring_at + r) % 16
        return (gx, (other // 8) * 8 + gy % 8, other % 8)

    z_ok = {-1: gz > 0, 0: None, 1: gz < NZ - 1}
    x_ok = {-1: gx > 0, 0: None, 1: gx < NX - 1}
    y_ok = {-2: gy > 1, -1: gy > 0, 0: None, 1: gy < NY - 1, 2: gy < NY - 2}

    def both(a, b):
        return b if a is None else a if b is None else a & b

    flat_ok = {(dz, dx): both(z_ok[dz], x_ok[dx]) for dz in z_ok for dx in x_ok}

    def there(o):
        return both(flat_ok[o[0], o[1]], y_ok[o[2]])

    def id_of(o):
        return (gx + o[1], gy + o[2], gz + o[0])

    def fetch(n, src, dst):
        copy = pltpu.make_async_copy(src, dst, in_sem.at[n])
        copy.start()
        return copy

    for ref in (NB, RB, HC, HZ, HX, YR):
        ref[...] = jnp.zeros(ref.shape, ref.dtype)
    get_co = fetch(0, co_in, NB.at[0, :, pl.ds(CENTRE, 1), :])
    get_cs = fetch(1, cs_in, cs)
    get_ws = fetch(2, ws_in, ws)
    get_mi = fetch(3, mi_in, mi)
    get_mg = fetch(4, mg_in, mg)
    get_tb = fetch(5, tb_in, tb)
    get_fg = fetch(6, fg_in, fg)
    get_vw = fetch(7, vw_in, vw)

    barrier = pltpu.get_barrier_semaphore()

    def greet(where):
        pl.semaphore_signal(barrier, inc=1, device_id=where, device_id_type=MESH)

    for o in NEAR[:36]:
        pl.when(there(o))(functools.partial(greet, id_of(o)))
    for r in (8, 7, 9, 6, 10, 5, 11, 4, 12, 3, 13, 2, 14, 1, 15):
        greet(ring_peer(r))
    for r in range(1, 32):
        greet(plane_peer(r))
    for o in NEAR[36:]:
        pl.when(there(o))(functools.partial(greet, id_of(o)))

    get_cs.wait()
    get_ws.wait()
    slot = cs[...]
    third = (slot * 11) >> 5
    comb = (ws[...] * 32 + (slot - 3 * third) * 9 + third).astype(F32)
    CT[...] = comb
    YS[0, 0:8, :] = comb
    YS[1, 0:8, :] = comb
    YS[:, 8:16, :] = jnp.zeros((2, 8, TY), F32)
    get_mi.wait()
    get_mg.wait()
    ends_at = iota((16, TY), 0)
    ends = jnp.where(iota((16, TY), 1) == jnp.where(ends_at == 0, TY - 1, 0), jnp.where(ends_at < 2, 1.0, 0.0), 0.0)
    ends = ends.astype(BF16)
    for a in range(4):
        rows = dot_nt(ends, (mi[...] if a == 0 else mg[a - 1]).reshape(ROWS, TY))
        YS[0, 8 + a : 9 + a, :] = rows[0:1]
        YS[1, 8 + a : 9 + a, :] = rows[1:2]
    for a in range(4):
        for z in range(TZ):
            whole = mi[z] if a == 0 else mg[a - 1, z]
            XS[0, a * 8 + z : a * 8 + z + 1, :] = whole.astype(F32)[TX - 1 : TX, :]
            XS[1, a * 8 + z : a * 8 + z + 1, :] = whole.astype(F32)[0:1, :]

    count_z = 3 - (gz == 0).astype(jnp.int32) - (gz == NZ - 1).astype(jnp.int32)
    count_x = 3 - (gx == 0).astype(jnp.int32) - (gx == NX - 1).astype(jnp.int32)
    count_y = jnp.minimum(gy, 2) + jnp.minimum(NY - 1 - gy, 2) + 1
    near_count = count_z * count_x * count_y - 1
    get_co.wait()
    pl.semaphore_wait(barrier, near_count + 46)

    def block_copy(buffer_from, row_from, buffer_to, row_to, send, recv, where):
        return pltpu.make_async_remote_copy(
            src_ref=buffer_from.at[:, pl.ds(row_from, 1), :],
            dst_ref=buffer_to.at[:, pl.ds(row_to, 1), :],
            send_sem=send, recv_sem=recv, device_id=where, device_id_type=MESH,
        )

    def spread_copy(k, o):
        u = index_of(*o)
        return block_copy(NB.at[k], CENTRE, NB.at[k], FIRST + 44 - u, nb_send.at[k], nb_recv.at[k], id_of(o))

    def gather_copy(k, o):
        u = index_of(*o)
        return block_copy(PB.at[k], FIRST + u, RB.at[k], FIRST + 44 - u, rb_send.at[k], rb_recv.at[k], id_of(o))

    def start(maker, k):
        for o in NEAR:
            pl.when(there(o))(maker(k, o).start)

    def all_blocks(buffer, k, send, recv, receive):
        for count in COUNTS:
            blocks = buffer.at[k, :, pl.ds(0, count), :]
            copy = pltpu.make_async_remote_copy(
                src_ref=blocks, dst_ref=blocks, send_sem=send.at[k], recv_sem=recv.at[k],
                device_id=mine, device_id_type=MESH,
            )
            pl.when(near_count == count)(copy.wait_recv if receive else copy.wait_send)

    def face_copies():
        result = []

        def add(n, src, dst, where, sends, gets):
            copy = pltpu.make_async_remote_copy(
                src_ref=src, dst_ref=dst, send_sem=face_send.at[n], recv_sem=face_recv.at[n],
                device_id=where, device_id_type=MESH,
            )
            result.append((copy, sends, gets))

        for f, side in ((0, 1), (1, -1)):
            add(f, YS.at[f], YR.at[f], id_of((0, 0, side)), y_ok[side], y_ok[-side])
        for f, side in ((0, 1), (1, -1)):
            at = TZ - 1 if f == 0 else 0
            where = id_of((side, 0, 0))
            add(2 + f, mi.at[at], HZ.at[f, 0], where, z_ok[side], z_ok[-side])
            add(4 + f, mg.at[:, at], HZ.at[f, pl.ds(1, 3)], where, z_ok[side], z_ok[-side])
            add(6 + f, CT, HC.at[f], where, z_ok[side], z_ok[-side])
        for f, side in ((0, 1), (1, -1)):
            where = id_of((0, side, 0))
            add(8 + f, XS.at[f], HX.at[f], where, x_ok[side], x_ok[-side])
            add(10 + f, CT, HC.at[2 + f], where, x_ok[side], x_ok[-side])
        return result

    def sum_copy(buffer, k, at, where, send, recv):
        return pltpu.make_async_remote_copy(
            src_ref=buffer.at[k, pl.ds(at, 1)], dst_ref=buffer.at[k, pl.ds(at, 1)],
            send_sem=send.at[k], recv_sem=recv.at[k], device_id=where, device_id_type=MESH,
        )

    def sum_all(buffer, k, count, send, recv):
        return pltpu.make_async_remote_copy(
            src_ref=buffer.at[k, pl.ds(0, count)], dst_ref=buffer.at[k, pl.ds(0, count)],
            send_sem=send.at[k], recv_sem=recv.at[k], device_id=plane_peer(1), device_id_type=MESH,
        )

    faces = face_copies()
    for copy, sends, _ in faces[:2]:
        pl.when(sends)(copy.start)
    start(spread_copy, 0)
    for copy, sends, _ in faces[2:]:
        pl.when(sends)(copy.start)

    which = iota((256, 256), 0).astype(F32)

    def picked(rows):
        hit = jnp.zeros((256, rows.shape[1]), F32)
        for k in range(8):
            hit = hit + jnp.where(rows[k : k + 1, :] == which[:, 0 : rows.shape[1]], 1.0, 0.0)
        return hit

    for c in range(3):
        MGS[c, 0:ROWS, :] = mg[c].astype(F32).reshape(ROWS, TY)
    own = picked(CT[...])
    PT2[:, 0:256] = own.astype(BF16)
    PT2[:, 384:640] = own.astype(BF16)
    own_t = own.T.astype(BF16)
    P2[0:256, 0:256] = own_t
    P2[0:256, 256:512] = own_t
    get_tb.wait()
    for c in range(3):
        for n in range(NW):
            TF[c * 16 + n : c * 16 + n + 1, :] = tb[n].astype(F32)[TY - 1 : TY, :]
            TF[c * 16 + 8 + n : c * 16 + 9 + n, :] = tb[n].astype(F32)[0:1, :]
    TF[48:128, :] = jnp.zeros((80, CP), F32)
    TE[...] = TF[...].astype(BF16)
    at_m, at_lane = iota((256, 128), 0), iota((256, 128), 1)
    for i, source in enumerate((
        jnp.where(at_lane < 32, at_lane + 224, -1),
        jnp.where((at_lane >= 32) & (at_lane < 64), at_lane - 32, -1),
        jnp.where((at_lane >= 64) & (at_lane < 72), (at_lane - 64) * TX + TX - 1, -1),
        jnp.where((at_lane >= 72) & (at_lane < 80), (at_lane - 72) * TX, -1),
    )):
        SEL[i] = jnp.where(at_m == source, 1.0, 0.0).astype(BF16)
    get_fg.wait()
    get_vw.wait()
    fixed = [fg[c].astype(F32) for c in range(3)]
    IFS[...] = 1.0 / (fixed[0] * fixed[0] + fixed[1] * fixed[1] + fixed[2] * fixed[2] + EDGE_SQUARED)
    WG[...] = jnp.zeros(WG.shape, BF16)
    for at in (0, 1, 10, 11):
        FZ[at] = jnp.zeros((TX, TY), F32)
    PB[...] = jnp.zeros(PB.shape, F32)

    for copy, _, gets in faces:
        pl.when(gets)(copy.wait_recv)
    all_blocks(NB, 0, nb_send, nb_recv, True)

    column = iota((1, 128), 1)
    shift = jnp.where(column < 32, -3.0, jnp.where(column < 64, 3.0, jnp.where(column < 72, -1.0, 1.0)))
    rows = None
    for i in range(4):
        part = dot(jnp.concatenate([HC[i], HC[i]], axis=0).astype(BF16), SEL[i])[0:8]
        rows = part if rows is None else rows + part
    halo = picked(rows + shift)
    PT2[:, 256:384] = halo.astype(BF16)
    PT2[:, 640:768] = halo.astype(BF16)
    halo_t = halo.T.astype(BF16)
    P2[256:384, 0:256] = halo_t
    P2[256:384, 256:512] = halo_t
    for c in range(3):
        MGS[c, 256:288, :] = HZ[0, 1 + c].astype(F32)
        MGS[c, 288:320, :] = HZ[1, 1 + c].astype(F32)
        MGS[c, 320:328, :] = HX[0, 8 + c * 8 : 16 + c * 8, :]
        MGS[c, 328:336, :] = HX[1, 8 + c * 8 : 16 + c * 8, :]
    YT[...] = jnp.zeros((128, 256), F32)
    for f in range(2):
        for c in range(3):
            YT[c * 16 : c * 16 + 16, :] = jnp.broadcast_to(YR[f, 9 + c : 10 + c, :], (16, 256))
        YT[48:49, :] = YR[f, 8:9, :]
        YC[f] = YT[...].T
        side = picked(YR[f, 0:8, :])
        PYT2[f, :, 0:256] = side.astype(BF16)
        PYT2[f, :, 256:512] = side.astype(BF16)
        side_t = side.T.astype(BF16)
        PY2[f, :, 0:256] = side_t
        PY2[f, :, 256:512] = side_t

    def forward(k):
        near = stacked(jnp.concatenate([NB[k, c, MAIN : MAIN + 32, :] for c in range(3)], axis=0))
        for n in range(NW):
            product = dot_nt(near, tb[n])
            high, low = split(product[0:96] + product[96:192])
            for c in range(3):
                BHL[c, n * 32 : n * 32 + 32, :] = high[c * 32 : c * 32 + 32]
                BHL[c, 256 + n * 32 : 288 + n * 32, :] = low[c * 32 : c * 32 + 32]
        total = None
        for c in range(3):
            part = dot(P2[0:336, :], BHL[c]) * MGS[c]
            total = part if total is None else total + part
        wide_blocks = stacked(jnp.concatenate([NB[k, c] for c in range(3)], axis=0))
        ends = dot_nt(wide_blocks, TE[...])
        ends = ends[0:192] + ends[192:384]
        columns = []
        for f in range(2):
            at = FIRST + 18 * f
            chosen = jnp.zeros((32, 128), F32)
            for c in range(3):
                chosen = jnp.where(lane // 16 == c, ends[c * 64 + at : c * 64 + at + 32], chosen)
            spread = jnp.concatenate(
                [jnp.where(lane % 16 == n + 8 * f, chosen, 0.0) for n in range(NW)], axis=0
            )
            columns.append(jnp.sum(dot(PY2[f], stacked(spread)) * YC[f], axis=1, keepdims=True))
        return total, columns

    total, columns = forward(0)
    WP[1:9] = mi[...].astype(F32) + total[0:256].reshape(TZ, TX, TY)
    for f, at in ((0, 0), (1, 9)):
        WP[at] = HZ[f, 0].astype(F32) + total[256 + 32 * f : 288 + 32 * f]
        WX[f] = HX[f, 0:8, :] + total[320 + 8 * f : 328 + 8 * f]
        WY[f] = jnp.broadcast_to(YC[f, :, 48:49] + columns[f], (256, 128))

    row_at = iota((TX, TY), 0)
    lane_at = iota((TX, TY), 1)

    def backward(k):
        def plane(z, energy):
            here = WP[z + 1]
            rows = pl.ds(pl.multiple_of(z * TX, TX), TX)
            back_x, on_x = pltpu.roll(here, 1, 0), pltpu.roll(here, TX - 1, 0)
            back_x = jnp.where(row_at == 0, WX[0, pl.ds(z, 1), :], back_x)
            on_x = jnp.where(row_at == TX - 1, WX[1, pl.ds(z, 1), :], on_x)
            back_y, on_y = pltpu.roll(here, 1, 1), pltpu.roll(here, TY - 1, 1)
            side = WY[0, rows, :]
            back_y = jnp.where(lane_at == 0, jnp.concatenate([side, side], axis=1), back_y)
            side = WY[1, rows, :]
            on_y = jnp.where(lane_at == TY - 1, jnp.concatenate([side, side], axis=1), on_y)
            grads = (WP[z + 2] - WP[z], on_x - back_x, on_y - back_y)
            fixed = [fg[c, z].astype(F32) for c in range(3)]
            inner = (grads[0] * fixed[0] + grads[1] * fixed[1] + grads[2] * fixed[2]) * 0.5
            moving = (grads[0] * grads[0] + grads[1] * grads[1] + grads[2] * grads[2]) * 0.25 + EDGE_SQUARED
            inverse = 1.0 / moving
            weight = vw[z].astype(F32)
            scaled = weight * inner * IFS[z] * inverse
            term = weight - inner * scaled
            other = 0.5 * scaled * inner * inverse
            flux = [other * grads[c] - scaled * fixed[c] for c in range(3)]
            FZ[z + 2] = flux[0]
            pulled = jnp.where(row_at == 0, 0.0, pltpu.roll(flux[1], 1, 0))
            pulled = pulled - jnp.where(row_at == TX - 1, 0.0, pltpu.roll(flux[1], TX - 1, 0))
            pulled = pulled + jnp.where(lane_at == 0, 0.0, pltpu.roll(flux[2], 1, 1))
            pulled = pulled - jnp.where(lane_at == TY - 1, 0.0, pltpu.roll(flux[2], TY - 1, 1))
            PU[z] = pulled
            PUX[0, pl.ds(z, 1), :] = -flux[1][0:1, :]
            PUX[1, pl.ds(z, 1), :] = flux[1][TX - 1 : TX, :]
            PYB[0, rows, :] = jnp.broadcast_to(-flux[2][:, 0:1], (TX, 128))
            PYB[1, rows, :] = jnp.broadcast_to(flux[2][:, TY - 1 : TY], (TX, 128))
            return energy + term

        energy = lax.fori_loop(0, TZ, plane, jnp.zeros((TX, TY), F32))
        energy = jnp.sum(energy, axis=0, keepdims=True)

        def put(block, rows, at):
            for c in range(3):
                high, low = split(block * MGS[c, pl.ds(at, rows), :])
                WG[c, pl.ds(at, rows), :] = high
                WG[c, pl.ds(at + 384, rows), :] = low

        def weigh(z, carry):
            put(PU[z] + FZ[z + 1] - FZ[z + 3], TX, pl.multiple_of(z * TX, TX))
            return carry

        lax.fori_loop(0, TZ, weigh, 0)
        put(-FZ[2], TX, 256)
        put(FZ[9], TX, 288)
        put(jnp.concatenate([PUX[0], PUX[1]], axis=0), 16, 320)
        for c in range(3):
            high, low = split(dot(PT2[...], WG[c]))
            for n in range(NW):
                GS[c * 32 : c * 32 + 32, n * 256 : n * 256 + 256] = high[n * 32 : n * 32 + 32]
                GS[96 + c * 32 : 128 + c * 32, n * 256 : n * 256 + 256] = low[n * 32 : n * 32 + 32]
        partial = dot(GS[...], tb[...].reshape(NW * TY, CP))
        partial = partial[0:96] + partial[96:192]
        for c in range(3):
            PB[k, c, MAIN : MAIN + 32, :] = partial[c * 32 : c * 32 + 32]
        for f in range(2):
            drawn = jnp.where(lane < 48, PYB[f] * YC[f], 0.0)
            back = dot(PYT2[f], stacked(drawn))
            chosen = jnp.zeros((32, 128), F32)
            for n in range(NW):
                chosen = jnp.where(lane % 16 == n + 8 * f, back[n * 32 : n * 32 + 32], chosen)
            blocks = jnp.concatenate([jnp.where(lane // 16 == c, chosen, 0.0) for c in range(3)], axis=0)
            ends = dot(stacked(blocks), TE[...])
            ends = ends[0:96] + ends[96:192]
            at = FIRST + 18 * f
            for c in range(3):
                PB[k, c, at : at + 32, :] = PB[k, c, at : at + 32, :] + ends[c * 32 : c * 32 + 32]
        return energy[:, 0:128] + energy[:, 128:256]

    def reduce_gradient(k, energy):
        start(gather_copy, k)
        for c in range(3):
            RB[k, c, CENTRE : CENTRE + 1, :] = PB[k, c, CENTRE : CENTRE + 1, :]
        all_blocks(RB, k, rb_send, rb_recv, True)
        gradient = [jnp.sum(RB[k, c], axis=0, keepdims=True) for c in range(3)]
        square = gradient[0] * gradient[0] + gradient[1] * gradient[1] + gradient[2] * gradient[2]
        energy = energy + pltpu.roll(energy, 64, 1)
        square = square + pltpu.roll(square, 64, 1)
        AP[k, pl.ds(plane_at, 1), :] = jnp.where(lane < 64, energy, square)
        for r in range(1, 32):
            sum_copy(AP, k, plane_at, plane_peer(r), ap_send, ap_recv).start()
        return gradient

    def pass_on(k):
        sum_all(AP, k, 31, ap_send, ap_recv).wait_recv()
        AZ[k, pl.ds(ring_at, 1), :] = jnp.sum(AP[k], axis=0, keepdims=True)
        for r in (8, 7, 9, 6, 10, 5, 11, 4, 12, 3, 13, 2, 14, 1, 15):
            sum_copy(AZ, k, ring_at, ring_peer(r), az_send, az_recv).start()

    def take_sum(k):
        sum_all(AZ, k, 15, az_send, az_recv).wait_recv()
        sums = jnp.sum(AZ[k], axis=0, keepdims=True)
        energy = jnp.sum(jnp.where(lane < 64, sums, 0.0), axis=1, keepdims=True)
        square = jnp.sum(jnp.where(lane < 64, 0.0, sums), axis=1, keepdims=True)
        devices = NX * NY * NZ
        step_size = STEP_LENGTH * lax.rsqrt(square * (1.0 / (devices * 3 * CP)) + 1e-06)
        return energy * (1.0 / (devices * TZ * TX * TY)), step_size

    energy = backward(0)
    first = reduce_gradient(0, energy)
    for c in range(3):
        NB[1, c, CENTRE : CENTRE + 1, :] = first[c]
    start(spread_copy, 1)
    pass_on(0)
    for copy, sends, _ in faces:
        pl.when(sends)(copy.wait_send)
    all_blocks(NB, 0, nb_send, nb_recv, False)
    all_blocks(NB, 1, nb_send, nb_recv, True)
    total, columns = forward(1)
    energy_0, size_0 = take_sum(0)
    WP[1:9] = WP[1:9] - size_0[0, 0] * total[0:256].reshape(TZ, TX, TY)
    for f, at in ((0, 0), (1, 9)):
        WP[at] = WP[at] - size_0 * total[256 + 32 * f : 288 + 32 * f]
        WX[f] = WX[f] - size_0 * total[320 + 8 * f : 328 + 8 * f]
        WY[f] = WY[f] - size_0 * columns[f]
    out_w[...] = WP[1:9]
    energy = backward(1)
    second = reduce_gradient(1, energy)
    all_blocks(RB, 0, rb_send, rb_recv, False)
    all_blocks(NB, 1, nb_send, nb_recv, False)
    sum_all(AP, 0, 31, ap_send, ap_recv).wait_send()
    sum_all(AZ, 0, 15, az_send, az_recv).wait_send()
    pass_on(1)
    all_blocks(RB, 1, rb_send, rb_recv, False)
    sum_all(AP, 1, 31, ap_send, ap_recv).wait_send()
    energy_1, size_1 = take_sum(1)
    sum_all(AZ, 1, 15, az_send, az_recv).wait_send()
    for c in range(3):
        out_c[c] = NB[0, c, CENTRE : CENTRE + 1, :] - size_0 * first[c] - size_1 * second[c]
    out_e[0] = energy_0[0, 0]
    out_e[1] = energy_1[0, 0]


def on_device(moving_image, moving_grad, fixed_grad, voxel_weight, coefficients, weight_table, ctrl_slot, weight_slot):
    whole = pl.BlockSpec(memory_space=pltpu.VMEM)
    vmem = pltpu.VMEM
    sem = pltpu.SemaphoreType.DMA
    new, warped, energies = pl.pallas_call(
        kernel,
        out_shape=(
            jax.ShapeDtypeStruct((3, 1, CP), F32),
            jax.ShapeDtypeStruct((TZ, TX, TY), F32),
            jax.ShapeDtypeStruct((2,), F32),
        ),
        in_specs=[pl.BlockSpec(memory_space=pltpu.HBM)] * 8,
        out_specs=(whole, whole, pl.BlockSpec(memory_space=pltpu.SMEM)),
        scratch_shapes=[
            vmem((TZ, TX, TY), BF16),
            vmem((3, TZ, TX, TY), BF16),
            vmem((3, TZ, TX, TY), BF16),
            vmem((TZ, TX, TY), BF16),
            vmem((NW, TY, CP), BF16),
            vmem((8, ROWS), jnp.int32),
            vmem((8, ROWS), jnp.int32),
            vmem((2, 3, 64, CP), F32),
            vmem((2, 3, 64, CP), F32),
            vmem((2, 3, 64, CP), F32),
            vmem((2, 32, 128), F32),
            vmem((2, 16, 128), F32),
            vmem((8, ROWS), F32),
            vmem((4, 8, ROWS), F32),
            vmem((4, ROWS, 128), BF16),
            vmem((2, 4, TX, TY), BF16),
            vmem((2, 32, TY), F32),
            vmem((2, 32, TY), F32),
            vmem((2, 16, TY), F32),
            vmem((2, 16, TY), F32),
            vmem((384, 512), BF16),
            vmem((256, 768), BF16),
            vmem((2, 256, 512), BF16),
            vmem((2, 256, 512), BF16),
            vmem((3, 336, TY), F32),
            vmem((2, 256, 128), F32),
            vmem((3, 512, TY), BF16),
            vmem((10, TX, TY), F32),
            vmem((2, 8, TY), F32),
            vmem((2, 256, 128), F32),
            vmem((TZ, TX, TY), F32),
            vmem((12, TX, TY), F32),
            vmem((TZ, TX, TY), F32),
            vmem((2, 8, TY), F32),
            vmem((2, 256, 128), F32),
            vmem((3, 768, TY), BF16),
            vmem((192, 2048), BF16),
            vmem((128, CP), F32),
            vmem((128, CP), BF16),
            vmem((128, 256), F32),
            sem((8,)), sem((2,)), sem((2,)), sem((2,)), sem((2,)),
            sem((12,)), sem((12,)), sem((2,)), sem((2,)), sem((2,)), sem((2,)),
        ],
        compiler_params=pltpu.CompilerParams(
            collective_id=0, has_side_effects=True, vmem_limit_bytes=63 * 1024 * 1024
        ),
    )(
        moving_image, moving_grad, fixed_grad, voxel_weight, coefficients.reshape(3, 1, CP), weight_table,
        ctrl_slot.reshape(ROWS, 8).T, weight_slot.reshape(ROWS, 8).T,
    )
    return new.reshape(1, 1, 1, 3, CP), warped, energies


def solution(mesh):
    in_specs = (
        P("gz", "gx", "gy"),
        P(None, "gz", "gx", "gy"),
        P(None, "gz", "gx", "gy"),
        P("gz", "gx", "gy"),
        P("gz", "gx", "gy", None, None),
        P(),
        P("gz", "gx", "gy", None, None),
        P("gz", "gx", "gy", None, None),
    )
    out_specs = (P("gz", "gx", "gy", None, None), P("gz", "gx", "gy"), P())
    return jax.shard_map(on_device, mesh=mesh, in_specs=in_specs, out_specs=out_specs, check_vma=False)
```

```python
import functools

import jax
import jax.numpy as jnp
from jax import lax
from jax.experimental import pallas as pl
from jax.experimental.pallas import tpu as pltpu
from jax.sharding import PartitionSpec as P

MESH = pl.DeviceIdType.MESH
F32 = jnp.float32
BF16 = jnp.bfloat16
EDGE_SQUARED = 0.05
STEP_LENGTH = 0.05
NX, NY, NZ = 4, 16, 8
TZ, TX, TY, CP, NW = 8, 32, 256, 128, 8
ROWS = TZ * TX
FIRST = 7
CENTRE = FIRST + 22
MAIN = FIRST + 9
UNROLL = 8


def split(x):
    high = x.astype(BF16)
    return high, (x - high.astype(F32)).astype(BF16)


def stacked(x):
    return jnp.concatenate(split(x), axis=0)


def dot(a, b):
    return jnp.dot(a, b, preferred_element_type=F32)


def dot_nt(a, b):
    return lax.dot_general(a, b, (((1,), (1,)), ((), ())), preferred_element_type=F32)


def iota(shape, dim):
    return lax.broadcasted_iota(jnp.int32, shape, dim)


NEAR = [
    (dz, dx, dy) for dy in (2, 1, -2, -1, 0) for dx in (-1, 1, 0) for dz in (0, -1, 1) if (dz, dx, dy) != (0, 0, 0)
]
REST = [o for o in NEAR if abs(o[2]) < 2]
PLANE = sorted(
    range(1, 32), key=lambda r: -(min(r // 8, 4 - r // 8) + min(r % 8 // 2, 4 - r % 8 // 2))
)
RING = (8, 7, 9, 6, 10, 5, 11, 4, 12, 3, 13, 2, 14, 1, 15)
COUNTS = sorted({a * b * c - 1 for a in (2, 3) for b in (2, 3) for c in (3, 4, 5)})


def kernel(
    mi_in, mg_in, fg_in, vw_in, co_in, tb_in, cs_in, ws_in,
    out_c, out_w, out_e,
    mi, mg, fg, vw, tb, cs, ws,
    NB, PB, RB, AP, AZ, CT, HC, SEL, HZ, HX, XS, YS, YR, P2, PT2, PY2, PYT2, MGS, YC, BHL,
    WP, WX, WY, IFS, FZ, PU, PUX, PYB, WG, GS, TF, TE, YT,
    in_sem, nb_send, nb_recv, rb_send, rb_recv, face_send, face_recv, ap_send, ap_recv, az_send, az_recv,
):
    gx, gy, gz = lax.axis_index("gx"), lax.axis_index("gy"), lax.axis_index("gz")
    lane = iota((1, 128), 1)
    plane_at = gx * 8 + gy % 8
    ring_at = (gy // 8) * 8 + gz

    mine = (gx, gy, gz)

    def plane_peer(r):
        other = (plane_at + r) % 32
        return (other // 8, (gy // 8) * 8 + other % 8, gz)

    def ring_peer(r):
        other = (ring_at + r) % 16
        return (gx, (other // 8) * 8 + gy % 8, other % 8)

    z_ok = {-1: gz > 0, 0: None, 1: gz < NZ - 1}
    x_ok = {-1: gx > 0, 0: None, 1: gx < NX - 1}
    side_y = {-1: gy > 0, 1: gy < NY - 1}
    toward = 1 - 2 * (gy // (NY // 2))
    out = jnp.where(gy < NY // 2, gy, NY - 1 - gy)
    y_ok = {-2: out > 1, -1: out > 0, 0: None, 1: None, 2: None}

    def both(a, b):
        return b if a is None else a if b is None else a & b

    flat_ok = {(dz, dx): both(z_ok[dz], x_ok[dx]) for dz in z_ok for dx in x_ok}

    def there(o):
        found = both(flat_ok[o[0], o[1]], y_ok[o[2]])
        return gx >= 0 if found is None else found

    def id_of(o):
        return (gx + o[1], gy + toward * o[2], gz + o[0])

    def index_of(o):
        return (toward * o[2] + 2) * 9 + ((o[0] + 1) * 3 + o[1] + 1)

    def fetch(n, src, dst):
        copy = pltpu.make_async_copy(src, dst, in_sem.at[n])
        copy.start()
        return copy

    for ref in (NB, RB, HC, HZ, HX, YR):
        ref[...] = jnp.zeros(ref.shape, ref.dtype)
    get_co = fetch(0, co_in, NB.at[0, :, pl.ds(CENTRE, 1), :])
    get_cs = fetch(1, cs_in, cs)
    get_ws = fetch(2, ws_in, ws)
    get_mi = fetch(3, mi_in, mi)
    get_mg = fetch(4, mg_in, mg)
    get_tb = fetch(5, tb_in, tb)
    get_fg = fetch(6, fg_in, fg)
    get_vw = fetch(7, vw_in, vw)

    barrier = pltpu.get_barrier_semaphore()

    def greet(where):
        pl.semaphore_signal(barrier, inc=1, device_id=where, device_id_type=MESH)

    for o in NEAR[:36]:
        pl.when(there(o))(functools.partial(greet, id_of(o)))
    for r in RING:
        greet(ring_peer(r))
    for r in PLANE:
        greet(plane_peer(r))
    for o in NEAR[36:]:
        pl.when(there(o))(functools.partial(greet, id_of(o)))

    get_cs.wait()
    get_ws.wait()
    slot = cs[...]
    third = (slot * 11) >> 5
    comb = (ws[...] * 32 + (slot - 3 * third) * 9 + third).astype(F32)
    CT[...] = comb
    YS[0, 0:8, :] = comb
    YS[1, 0:8, :] = comb
    YS[:, 8:16, :] = jnp.zeros((2, 8, TY), F32)
    get_mi.wait()
    get_mg.wait()
    ends_at = iota((16, TY), 0)
    ends = jnp.where(iota((16, TY), 1) == jnp.where(ends_at == 0, TY - 1, 0), jnp.where(ends_at < 2, 1.0, 0.0), 0.0)
    ends = ends.astype(BF16)
    for a in range(4):
        rows = dot_nt(ends, (mi[...] if a == 0 else mg[a - 1]).reshape(ROWS, TY))
        YS[0, 8 + a : 9 + a, :] = rows[0:1]
        YS[1, 8 + a : 9 + a, :] = rows[1:2]
    for a in range(4):
        for z in range(TZ):
            whole = mi[z] if a == 0 else mg[a - 1, z]
            XS[0, a * 8 + z : a * 8 + z + 1, :] = whole.astype(F32)[TX - 1 : TX, :]
            XS[1, a * 8 + z : a * 8 + z + 1, :] = whole.astype(F32)[0:1, :]

    count_z = 3 - (gz == 0).astype(jnp.int32) - (gz == NZ - 1).astype(jnp.int32)
    count_x = 3 - (gx == 0).astype(jnp.int32) - (gx == NX - 1).astype(jnp.int32)
    count_y = jnp.minimum(gy, 2) + jnp.minimum(NY - 1 - gy, 2) + 1
    near_count = count_z * count_x * count_y - 1
    get_co.wait()
    pl.semaphore_wait(barrier, near_count + 46)

    def block_copy(buffer_from, row_from, buffer_to, row_to, send, recv, where):
        return pltpu.make_async_remote_copy(
            src_ref=buffer_from.at[:, pl.ds(row_from, 1), :],
            dst_ref=buffer_to.at[:, pl.ds(row_to, 1), :],
            send_sem=send, recv_sem=recv, device_id=where, device_id_type=MESH,
        )

    def spread_copy(k, o):
        u = index_of(o)
        return block_copy(NB.at[k], CENTRE, NB.at[k], FIRST + 44 - u, nb_send.at[k], nb_recv.at[k], id_of(o))

    def gather_copy(k, o):
        u = index_of(o)
        return block_copy(PB.at[k], FIRST + u, RB.at[k], FIRST + 44 - u, rb_send.at[k], rb_recv.at[k], id_of(o))

    def start(maker, k, offsets=NEAR):
        for o in offsets:
            pl.when(there(o))(maker(k, o).start)

    def all_blocks(buffer, k, send, recv, receive):
        for count in COUNTS:
            blocks = buffer.at[k, :, pl.ds(0, count), :]
            copy = pltpu.make_async_remote_copy(
                src_ref=blocks, dst_ref=blocks, send_sem=send.at[k], recv_sem=recv.at[k],
                device_id=mine, device_id_type=MESH,
            )
            pl.when(near_count == count)(copy.wait_recv if receive else copy.wait_send)

    def face_copies():
        result = []

        def add(n, src, dst, where, sends, gets):
            copy = pltpu.make_async_remote_copy(
                src_ref=src, dst_ref=dst, send_sem=face_send.at[n], recv_sem=face_recv.at[n],
                device_id=where, device_id_type=MESH,
            )
            result.append((copy, sends, gets))

        for f, side in ((0, 1), (1, -1)):
            add(f, YS.at[f], YR.at[f], (gx, gy + side, gz), side_y[side], side_y[-side])
        for f, side in ((0, 1), (1, -1)):
            at = TZ - 1 if f == 0 else 0
            where = id_of((side, 0, 0))
            add(2 + f, mi.at[at], HZ.at[f, 0], where, z_ok[side], z_ok[-side])
            add(4 + f, mg.at[:, at], HZ.at[f, pl.ds(1, 3)], where, z_ok[side], z_ok[-side])
            add(6 + f, CT, HC.at[f], where, z_ok[side], z_ok[-side])
        for f, side in ((0, 1), (1, -1)):
            where = id_of((0, side, 0))
            add(8 + f, XS.at[f], HX.at[f], where, x_ok[side], x_ok[-side])
            add(10 + f, CT, HC.at[2 + f], where, x_ok[side], x_ok[-side])
        return result

    def sum_copy(buffer, k, at, where, send, recv):
        return pltpu.make_async_remote_copy(
            src_ref=buffer.at[k, pl.ds(at, 1)], dst_ref=buffer.at[k, pl.ds(at, 1)],
            send_sem=send.at[k], recv_sem=recv.at[k], device_id=where, device_id_type=MESH,
        )

    def sum_all(buffer, k, count, send, recv):
        return pltpu.make_async_remote_copy(
            src_ref=buffer.at[k, pl.ds(0, count)], dst_ref=buffer.at[k, pl.ds(0, count)],
            send_sem=send.at[k], recv_sem=recv.at[k], device_id=plane_peer(1), device_id_type=MESH,
        )

    faces = face_copies()
    for copy, sends, _ in faces[:2]:
        pl.when(sends)(copy.start)
    start(spread_copy, 0)
    for copy, sends, _ in faces[2:]:
        pl.when(sends)(copy.start)

    which = iota((256, 256), 0).astype(F32)

    def picked(rows):
        hit = jnp.zeros((256, rows.shape[1]), F32)
        for k in range(8):
            hit = hit + jnp.where(rows[k : k + 1, :] == which[:, 0 : rows.shape[1]], 1.0, 0.0)
        return hit

    for c in range(3):
        MGS[c, 0:ROWS, :] = mg[c].astype(F32).reshape(ROWS, TY)
    own = picked(CT[...])
    PT2[:, 0:256] = own.astype(BF16)
    PT2[:, 384:640] = own.astype(BF16)
    own_t = own.T.astype(BF16)
    P2[0:256, 0:256] = own_t
    P2[0:256, 256:512] = own_t
    get_tb.wait()
    for c in range(3):
        for n in range(NW):
            TF[c * 16 + n : c * 16 + n + 1, :] = tb[n].astype(F32)[TY - 1 : TY, :]
            TF[c * 16 + 8 + n : c * 16 + 9 + n, :] = tb[n].astype(F32)[0:1, :]
    TF[48:128, :] = jnp.zeros((80, CP), F32)
    TE[...] = TF[...].astype(BF16)
    at_m, at_lane = iota((256, 128), 0), iota((256, 128), 1)
    for i, source in enumerate((
        jnp.where(at_lane < 32, at_lane + 224, -1),
        jnp.where((at_lane >= 32) & (at_lane < 64), at_lane - 32, -1),
        jnp.where((at_lane >= 64) & (at_lane < 72), (at_lane - 64) * TX + TX - 1, -1),
        jnp.where((at_lane >= 72) & (at_lane < 80), (at_lane - 72) * TX, -1),
    )):
        SEL[i] = jnp.where(at_m == source, 1.0, 0.0).astype(BF16)
    get_fg.wait()
    get_vw.wait()
    fixed = [fg[c].astype(F32) for c in range(3)]
    IFS[...] = 1.0 / (fixed[0] * fixed[0] + fixed[1] * fixed[1] + fixed[2] * fixed[2] + EDGE_SQUARED)
    WG[...] = jnp.zeros(WG.shape, BF16)
    for at in (0, 1, 10, 11):
        FZ[at] = jnp.zeros((TX, TY), F32)
    PB[...] = jnp.zeros(PB.shape, F32)

    for copy, _, gets in faces[2:]:
        pl.when(gets)(copy.wait_recv)

    column = iota((1, 128), 1)
    shift = jnp.where(column < 32, -3.0, jnp.where(column < 64, 3.0, jnp.where(column < 72, -1.0, 1.0)))
    rows = None
    for i in range(4):
        part = dot(jnp.concatenate([HC[i], HC[i]], axis=0).astype(BF16), SEL[i])[0:8]
        rows = part if rows is None else rows + part
    halo = picked(rows + shift)
    PT2[:, 256:384] = halo.astype(BF16)
    PT2[:, 640:768] = halo.astype(BF16)
    halo_t = halo.T.astype(BF16)
    P2[256:384, 0:256] = halo_t
    P2[256:384, 256:512] = halo_t
    for c in range(3):
        MGS[c, 256:288, :] = HZ[0, 1 + c].astype(F32)
        MGS[c, 288:320, :] = HZ[1, 1 + c].astype(F32)
        MGS[c, 320:328, :] = HX[0, 8 + c * 8 : 16 + c * 8, :]
        MGS[c, 328:336, :] = HX[1, 8 + c * 8 : 16 + c * 8, :]
    YT[...] = jnp.zeros((128, 256), F32)
    for copy, _, gets in faces[:2]:
        pl.when(gets)(copy.wait_recv)
    for f in range(2):
        for c in range(3):
            YT[c * 16 : c * 16 + 16, :] = jnp.broadcast_to(YR[f, 9 + c : 10 + c, :], (16, 256))
        YT[48:49, :] = YR[f, 8:9, :]
        YC[f] = YT[...].T
        side = picked(YR[f, 0:8, :])
        PYT2[f, :, 0:256] = side.astype(BF16)
        PYT2[f, :, 256:512] = side.astype(BF16)
        side_t = side.T.astype(BF16)
        PY2[f, :, 0:256] = side_t
        PY2[f, :, 256:512] = side_t

    all_blocks(NB, 0, nb_send, nb_recv, True)

    def forward(k):
        near = stacked(jnp.concatenate([NB[k, c, MAIN : MAIN + 32, :] for c in range(3)], axis=0))
        for n in range(NW):
            product = dot_nt(near, tb[n])
            high, low = split(product[0:96] + product[96:192])
            for c in range(3):
                BHL[c, n * 32 : n * 32 + 32, :] = high[c * 32 : c * 32 + 32]
                BHL[c, 256 + n * 32 : 288 + n * 32, :] = low[c * 32 : c * 32 + 32]
        total = None
        for c in range(3):
            part = dot(P2[0:336, :], BHL[c]) * MGS[c]
            total = part if total is None else total + part
        wide_blocks = stacked(jnp.concatenate([NB[k, c] for c in range(3)], axis=0))
        ends = dot_nt(wide_blocks, TE[...])
        ends = ends[0:192] + ends[192:384]
        columns = []
        for f in range(2):
            at = FIRST + 18 * f
            chosen = jnp.zeros((32, 128), F32)
            for c in range(3):
                chosen = jnp.where(lane // 16 == c, ends[c * 64 + at : c * 64 + at + 32], chosen)
            spread = jnp.concatenate(
                [jnp.where(lane % 16 == n + 8 * f, chosen, 0.0) for n in range(NW)], axis=0
            )
            columns.append(jnp.sum(dot(PY2[f], stacked(spread)) * YC[f], axis=1, keepdims=True))
        return total, columns

    total, columns = forward(0)
    WP[1:9] = mi[...].astype(F32) + total[0:256].reshape(TZ, TX, TY)
    for f, at in ((0, 0), (1, 9)):
        WP[at] = HZ[f, 0].astype(F32) + total[256 + 32 * f : 288 + 32 * f]
        WX[f] = HX[f, 0:8, :] + total[320 + 8 * f : 328 + 8 * f]
        WY[f] = jnp.broadcast_to(YC[f, :, 48:49] + columns[f], (256, 128))

    row_at = iota((TX, TY), 0)
    lane_at = iota((TX, TY), 1)

    def backward(k):
        def plane(z, energy):
            here = WP[z + 1]
            rows = pl.ds(pl.multiple_of(z * TX, TX), TX)
            back_x, on_x = pltpu.roll(here, 1, 0), pltpu.roll(here, TX - 1, 0)
            back_x = jnp.where(row_at == 0, WX[0, pl.ds(z, 1), :], back_x)
            on_x = jnp.where(row_at == TX - 1, WX[1, pl.ds(z, 1), :], on_x)
            back_y, on_y = pltpu.roll(here, 1, 1), pltpu.roll(here, TY - 1, 1)
            side = WY[0, rows, :]
            back_y = jnp.where(lane_at == 0, jnp.concatenate([side, side], axis=1), back_y)
            side = WY[1, rows, :]
            on_y = jnp.where(lane_at == TY - 1, jnp.concatenate([side, side], axis=1), on_y)
            grads = (WP[z + 2] - WP[z], on_x - back_x, on_y - back_y)
            fixed = [fg[c, z].astype(F32) for c in range(3)]
            inner = (grads[0] * fixed[0] + grads[1] * fixed[1] + grads[2] * fixed[2]) * 0.5
            moving = (grads[0] * grads[0] + grads[1] * grads[1] + grads[2] * grads[2]) * 0.25 + EDGE_SQUARED
            inverse = 1.0 / moving
            weight = vw[z].astype(F32)
            scaled = weight * inner * IFS[z] * inverse
            term = weight - inner * scaled
            other = 0.5 * scaled * inner * inverse
            flux = [other * grads[c] - scaled * fixed[c] for c in range(3)]
            FZ[z + 2] = flux[0]
            pulled = jnp.where(row_at == 0, 0.0, pltpu.roll(flux[1], 1, 0))
            pulled = pulled - jnp.where(row_at == TX - 1, 0.0, pltpu.roll(flux[1], TX - 1, 0))
            pulled = pulled + jnp.where(lane_at == 0, 0.0, pltpu.roll(flux[2], 1, 1))
            pulled = pulled - jnp.where(lane_at == TY - 1, 0.0, pltpu.roll(flux[2], TY - 1, 1))
            PU[z] = pulled
            PUX[0, pl.ds(z, 1), :] = -flux[1][0:1, :]
            PUX[1, pl.ds(z, 1), :] = flux[1][TX - 1 : TX, :]
            PYB[0, rows, :] = jnp.broadcast_to(-flux[2][:, 0:1], (TX, 128))
            PYB[1, rows, :] = jnp.broadcast_to(flux[2][:, TY - 1 : TY], (TX, 128))
            return energy + term

        energy = lax.fori_loop(0, TZ, plane, jnp.zeros((TX, TY), F32), unroll=UNROLL)
        energy = jnp.sum(energy, axis=0, keepdims=True)
        for f in range(2):
            drawn = jnp.where(lane < 48, PYB[f] * YC[f], 0.0)
            back = dot(PYT2[f], stacked(drawn))
            chosen = jnp.zeros((32, 128), F32)
            for n in range(NW):
                chosen = jnp.where(lane % 16 == n + 8 * f, back[n * 32 : n * 32 + 32], chosen)
            blocks = jnp.concatenate([jnp.where(lane // 16 == c, chosen, 0.0) for c in range(3)], axis=0)
            ends = dot(stacked(blocks), TE[...])
            ends = ends[0:96] + ends[96:192]
            at = FIRST + 18 * f
            for c in range(3):
                PB[k, c, at : at + 32, :] = PB[k, c, at : at + 32, :] + ends[c * 32 : c * 32 + 32]
        start(gather_copy, k, [o for o in NEAR if abs(o[2]) == 2])

        def put(block, rows, at):
            for c in range(3):
                high, low = split(block * MGS[c, pl.ds(at, rows), :])
                WG[c, pl.ds(at, rows), :] = high
                WG[c, pl.ds(at + 384, rows), :] = low

        def weigh(z, carry):
            put(PU[z] + FZ[z + 1] - FZ[z + 3], TX, pl.multiple_of(z * TX, TX))
            return carry

        lax.fori_loop(0, TZ, weigh, 0, unroll=UNROLL)
        put(-FZ[2], TX, 256)
        put(FZ[9], TX, 288)
        put(jnp.concatenate([PUX[0], PUX[1]], axis=0), 16, 320)
        for c in range(3):
            high, low = split(dot(PT2[...], WG[c]))
            for n in range(NW):
                GS[c * 32 : c * 32 + 32, n * 256 : n * 256 + 256] = high[n * 32 : n * 32 + 32]
                GS[96 + c * 32 : 128 + c * 32, n * 256 : n * 256 + 256] = low[n * 32 : n * 32 + 32]
        partial = dot(GS[...], tb[...].reshape(NW * TY, CP))
        partial = partial[0:96] + partial[96:192]
        for c in range(3):
            PB[k, c, MAIN : MAIN + 27, :] = PB[k, c, MAIN : MAIN + 27, :] + partial[c * 32 : c * 32 + 27]
        return energy[:, 0:128] + energy[:, 128:256]

    def reduce_gradient(k, energy):
        start(gather_copy, k, REST)
        for c in range(3):
            RB[k, c, CENTRE : CENTRE + 1, :] = PB[k, c, CENTRE : CENTRE + 1, :]
        all_blocks(RB, k, rb_send, rb_recv, True)
        gradient = [jnp.sum(RB[k, c], axis=0, keepdims=True) for c in range(3)]
        square = gradient[0] * gradient[0] + gradient[1] * gradient[1] + gradient[2] * gradient[2]
        energy = energy + pltpu.roll(energy, 64, 1)
        square = square + pltpu.roll(square, 64, 1)
        AP[k, pl.ds(plane_at, 1), :] = jnp.where(lane < 64, energy, square)
        for r in PLANE:
            sum_copy(AP, k, plane_at, plane_peer(r), ap_send, ap_recv).start()
        return gradient

    def pass_on(k):
        sum_all(AP, k, 31, ap_send, ap_recv).wait_recv()
        AZ[k, pl.ds(ring_at, 1), :] = jnp.sum(AP[k], axis=0, keepdims=True)
        for r in RING:
            sum_copy(AZ, k, ring_at, ring_peer(r), az_send, az_recv).start()

    def take_sum(k):
        sum_all(AZ, k, 15, az_send, az_recv).wait_recv()
        sums = jnp.sum(AZ[k], axis=0, keepdims=True)
        energy = jnp.sum(jnp.where(lane < 64, sums, 0.0), axis=1, keepdims=True)
        square = jnp.sum(jnp.where(lane < 64, 0.0, sums), axis=1, keepdims=True)
        devices = NX * NY * NZ
        step_size = STEP_LENGTH * lax.rsqrt(square * (1.0 / (devices * 3 * CP)) + 1e-06)
        return energy * (1.0 / (devices * TZ * TX * TY)), step_size

    energy = backward(0)
    first = reduce_gradient(0, energy)
    for c in range(3):
        NB[1, c, CENTRE : CENTRE + 1, :] = first[c]
    start(spread_copy, 1)
    pass_on(0)
    for copy, sends, _ in faces:
        pl.when(sends)(copy.wait_send)
    all_blocks(NB, 0, nb_send, nb_recv, False)
    all_blocks(NB, 1, nb_send, nb_recv, True)
    total, columns = forward(1)
    energy_0, size_0 = take_sum(0)
    WP[1:9] = WP[1:9] - size_0[0, 0] * total[0:256].reshape(TZ, TX, TY)
    for f, at in ((0, 0), (1, 9)):
        WP[at] = WP[at] - size_0 * total[256 + 32 * f : 288 + 32 * f]
        WX[f] = WX[f] - size_0 * total[320 + 8 * f : 328 + 8 * f]
        WY[f] = WY[f] - size_0 * columns[f]
    out_w[...] = WP[1:9]
    energy = backward(1)
    second = reduce_gradient(1, energy)
    all_blocks(RB, 0, rb_send, rb_recv, False)
    all_blocks(NB, 1, nb_send, nb_recv, False)
    sum_all(AP, 0, 31, ap_send, ap_recv).wait_send()
    sum_all(AZ, 0, 15, az_send, az_recv).wait_send()
    pass_on(1)
    all_blocks(RB, 1, rb_send, rb_recv, False)
    sum_all(AP, 1, 31, ap_send, ap_recv).wait_send()
    energy_1, size_1 = take_sum(1)
    sum_all(AZ, 1, 15, az_send, az_recv).wait_send()
    for c in range(3):
        out_c[c] = NB[0, c, CENTRE : CENTRE + 1, :] - size_0 * first[c] - size_1 * second[c]
    out_e[0] = energy_0[0, 0]
    out_e[1] = energy_1[0, 0]


def on_device(moving_image, moving_grad, fixed_grad, voxel_weight, coefficients, weight_table, ctrl_slot, weight_slot):
    whole = pl.BlockSpec(memory_space=pltpu.VMEM)
    vmem = pltpu.VMEM
    sem = pltpu.SemaphoreType.DMA
    new, warped, energies = pl.pallas_call(
        kernel,
        out_shape=(
            jax.ShapeDtypeStruct((3, 1, CP), F32),
            jax.ShapeDtypeStruct((TZ, TX, TY), F32),
            jax.ShapeDtypeStruct((2,), F32),
        ),
        in_specs=[pl.BlockSpec(memory_space=pltpu.HBM)] * 8,
        out_specs=(whole, whole, pl.BlockSpec(memory_space=pltpu.SMEM)),
        scratch_shapes=[
            vmem((TZ, TX, TY), BF16),
            vmem((3, TZ, TX, TY), BF16),
            vmem((3, TZ, TX, TY), BF16),
            vmem((TZ, TX, TY), BF16),
            vmem((NW, TY, CP), BF16),
            vmem((8, ROWS), jnp.int32),
            vmem((8, ROWS), jnp.int32),
            vmem((2, 3, 64, CP), F32),
            vmem((2, 3, 64, CP), F32),
            vmem((2, 3, 64, CP), F32),
            vmem((2, 32, 128), F32),
            vmem((2, 16, 128), F32),
            vmem((8, ROWS), F32),
            vmem((4, 8, ROWS), F32),
            vmem((4, ROWS, 128), BF16),
            vmem((2, 4, TX, TY), BF16),
            vmem((2, 32, TY), F32),
            vmem((2, 32, TY), F32),
            vmem((2, 16, TY), F32),
            vmem((2, 16, TY), F32),
            vmem((384, 512), BF16),
            vmem((256, 768), BF16),
            vmem((2, 256, 512), BF16),
            vmem((2, 256, 512), BF16),
            vmem((3, 336, TY), F32),
            vmem((2, 256, 128), F32),
            vmem((3, 512, TY), BF16),
            vmem((10, TX, TY), F32),
            vmem((2, 8, TY), F32),
            vmem((2, 256, 128), F32),
            vmem((TZ, TX, TY), F32),
            vmem((12, TX, TY), F32),
            vmem((TZ, TX, TY), F32),
            vmem((2, 8, TY), F32),
            vmem((2, 256, 128), F32),
            vmem((3, 768, TY), BF16),
            vmem((192, 2048), BF16),
            vmem((128, CP), F32),
            vmem((128, CP), BF16),
            vmem((128, 256), F32),
            sem((8,)), sem((2,)), sem((2,)), sem((2,)), sem((2,)),
            sem((12,)), sem((12,)), sem((2,)), sem((2,)), sem((2,)), sem((2,)),
        ],
        compiler_params=pltpu.CompilerParams(
            collective_id=0, has_side_effects=True, vmem_limit_bytes=63 * 1024 * 1024
        ),
    )(
        moving_image, moving_grad, fixed_grad, voxel_weight, coefficients.reshape(3, 1, CP), weight_table,
        ctrl_slot.reshape(ROWS, 8).T, weight_slot.reshape(ROWS, 8).T,
    )
    return new.reshape(1, 1, 1, 3, CP), warped, energies


def solution(mesh):
    in_specs = (
        P("gz", "gx", "gy"),
        P(None, "gz", "gx", "gy"),
        P(None, "gz", "gx", "gy"),
        P("gz", "gx", "gy"),
        P("gz", "gx", "gy", None, None),
        P(),
        P("gz", "gx", "gy", None, None),
        P("gz", "gx", "gy", None, None),
    )
    out_specs = (P("gz", "gx", "gy", None, None), P("gz", "gx", "gy"), P())
    return jax.shard_map(on_device, mesh=mesh, in_specs=in_specs, out_specs=out_specs, check_vma=False)
```

```python
import functools

import jax
import jax.numpy as jnp
from jax import lax
from jax.experimental import pallas as pl
from jax.experimental.pallas import tpu as pltpu
from jax.sharding import PartitionSpec as P

MESH = pl.DeviceIdType.MESH
F32 = jnp.float32
BF16 = jnp.bfloat16
EDGE_SQUARED = 0.05
STEP_LENGTH = 0.05
NX, NY, NZ = 4, 16, 8
TZ, TX, TY, CP, NW = 8, 32, 256, 128, 8
ROWS = TZ * TX
FIRST = 7
CENTRE = FIRST + 22
MAIN = FIRST + 9
UNROLL = 8


def split(x):
    high = x.astype(BF16)
    return high, (x - high.astype(F32)).astype(BF16)


def stacked(x):
    return jnp.concatenate(split(x), axis=0)


def dot(a, b):
    return jnp.dot(a, b, preferred_element_type=F32)


def dot_nt(a, b):
    return lax.dot_general(a, b, (((1,), (1,)), ((), ())), preferred_element_type=F32)


def iota(shape, dim):
    return lax.broadcasted_iota(jnp.int32, shape, dim)


NEAR = [
    (dz, dx, dy) for dy in (2, 1, -2, -1, 0) for dx in (-1, 1, 0) for dz in (0, -1, 1) if (dz, dx, dy) != (0, 0, 0)
]
REST = [o for o in NEAR if abs(o[2]) < 2]
PLANE = sorted(
    range(1, 32), key=lambda r: -(min(r // 8, 4 - r // 8) + min(r % 8 // 2, 4 - r % 8 // 2))
)
RING = (8, 7, 9, 6, 10, 5, 11, 4, 12, 3, 13, 2, 14, 1, 15)
COUNTS = sorted({a * b * c - 1 for a in (2, 3) for b in (2, 3) for c in (3, 4, 5)})


def kernel(
    mi_in, mg_in, fg_in, vw_in, co_in, tb_in, cs_in, ws_in,
    out_c, out_w, out_e,
    mi, mg, fg, vw, tb, cs, ws,
    NB, PB, RB, AP, AZ, CT, HC, SEL, HZ, HX, XS, YS, YR, P2, PT2, PY2, PYT2, MGS, YC, BHL,
    WP, WX, WY, IFS, FZ, PU, PUX, PYB, WG, GS, TF, TE, YT,
    in_sem, nb_send, nb_recv, rb_send, rb_recv, face_send, face_recv, ap_send, ap_recv, az_send, az_recv,
):
    gx, gy, gz = lax.axis_index("gx"), lax.axis_index("gy"), lax.axis_index("gz")
    lane = iota((1, 128), 1)
    plane_at = gx * 8 + gy % 8
    ring_at = (gy // 8) * 8 + gz

    mine = (gx, gy, gz)

    def plane_peer(r):
        other = (plane_at + r) % 32
        return (other // 8, (gy // 8) * 8 + other % 8, gz)

    def ring_peer(r):
        other = (ring_at + r) % 16
        return (gx, (other // 8) * 8 + gy % 8, other % 8)

    z_ok = {-1: gz > 0, 0: None, 1: gz < NZ - 1}
    x_ok = {-1: gx > 0, 0: None, 1: gx < NX - 1}
    side_y = {-1: gy > 0, 1: gy < NY - 1}
    toward = 1 - 2 * (gy // (NY // 2))
    out = jnp.where(gy < NY // 2, gy, NY - 1 - gy)
    y_ok = {-2: out > 1, -1: out > 0, 0: None, 1: None, 2: None}

    def both(a, b):
        return b if a is None else a if b is None else a & b

    flat_ok = {(dz, dx): both(z_ok[dz], x_ok[dx]) for dz in z_ok for dx in x_ok}

    def there(o):
        found = both(flat_ok[o[0], o[1]], y_ok[o[2]])
        return gx >= 0 if found is None else found

    def id_of(o):
        return (gx + o[1], gy + toward * o[2], gz + o[0])

    def index_of(o):
        return (toward * o[2] + 2) * 9 + ((o[0] + 1) * 3 + o[1] + 1)

    def fetch(n, src, dst):
        copy = pltpu.make_async_copy(src, dst, in_sem.at[n])
        copy.start()
        return copy

    for ref in (NB, RB, HC, HZ, HX, YR):
        ref[...] = jnp.zeros(ref.shape, ref.dtype)
    get_co = fetch(0, co_in, NB.at[0, :, pl.ds(CENTRE, 1), :])
    get_cs = fetch(1, cs_in, cs)
    get_ws = fetch(2, ws_in, ws)
    get_mi = fetch(3, mi_in, mi)
    get_mg = fetch(4, mg_in, mg)
    get_tb = fetch(5, tb_in, tb)
    get_fg = fetch(6, fg_in, fg)
    get_vw = fetch(7, vw_in, vw)

    barrier = pltpu.get_barrier_semaphore()

    def greet(where):
        pl.semaphore_signal(barrier, inc=1, device_id=where, device_id_type=MESH)

    for o in NEAR[:36]:
        pl.when(there(o))(functools.partial(greet, id_of(o)))
    for r in RING:
        greet(ring_peer(r))
    for r in PLANE:
        greet(plane_peer(r))
    for o in NEAR[36:]:
        pl.when(there(o))(functools.partial(greet, id_of(o)))

    get_cs.wait()
    get_ws.wait()
    slot = cs[...]
    third = (slot * 11) >> 5
    comb = (ws[...] * 32 + (slot - 3 * third) * 9 + third).astype(F32)
    CT[...] = comb
    YS[0, 0:8, :] = comb
    YS[1, 0:8, :] = comb
    YS[:, 8:16, :] = jnp.zeros((2, 8, TY), F32)
    get_mi.wait()
    get_mg.wait()
    ends_at = iota((16, TY), 0)
    ends = jnp.where(iota((16, TY), 1) == jnp.where(ends_at == 0, TY - 1, 0), jnp.where(ends_at < 2, 1.0, 0.0), 0.0)
    ends = ends.astype(BF16)
    for a in range(4):
        rows = dot_nt(ends, (mi[...] if a == 0 else mg[a - 1]).reshape(ROWS, TY))
        YS[0, 8 + a : 9 + a, :] = rows[0:1]
        YS[1, 8 + a : 9 + a, :] = rows[1:2]
    for a in range(4):
        for z in range(TZ):
            whole = mi[z] if a == 0 else mg[a - 1, z]
            XS[0, a * 8 + z : a * 8 + z + 1, :] = whole.astype(F32)[TX - 1 : TX, :]
            XS[1, a * 8 + z : a * 8 + z + 1, :] = whole.astype(F32)[0:1, :]

    count_z = 3 - (gz == 0).astype(jnp.int32) - (gz == NZ - 1).astype(jnp.int32)
    count_x = 3 - (gx == 0).astype(jnp.int32) - (gx == NX - 1).astype(jnp.int32)
    count_y = jnp.minimum(gy, 2) + jnp.minimum(NY - 1 - gy, 2) + 1
    near_count = count_z * count_x * count_y - 1
    get_co.wait()
    pl.semaphore_wait(barrier, near_count + 46)

    def block_copy(buffer_from, row_from, buffer_to, row_to, send, recv, where):
        return pltpu.make_async_remote_copy(
            src_ref=buffer_from.at[:, pl.ds(row_from, 1), :],
            dst_ref=buffer_to.at[:, pl.ds(row_to, 1), :],
            send_sem=send, recv_sem=recv, device_id=where, device_id_type=MESH,
        )

    def spread_copy(k, o):
        u = index_of(o)
        return block_copy(NB.at[k], CENTRE, NB.at[k], FIRST + 44 - u, nb_send.at[k], nb_recv.at[k], id_of(o))

    def gather_copy(k, o):
        u = index_of(o)
        return block_copy(PB.at[k], FIRST + u, RB.at[k], FIRST + 44 - u, rb_send.at[k], rb_recv.at[k], id_of(o))

    def start(maker, k, offsets=NEAR):
        for o in offsets:
            pl.when(there(o))(maker(k, o).start)

    def all_blocks(buffer, k, send, recv, receive):
        for count in COUNTS:
            blocks = buffer.at[k, :, pl.ds(0, count), :]
            copy = pltpu.make_async_remote_copy(
                src_ref=blocks, dst_ref=blocks, send_sem=send.at[k], recv_sem=recv.at[k],
                device_id=mine, device_id_type=MESH,
            )
            pl.when(near_count == count)(copy.wait_recv if receive else copy.wait_send)

    def face_copies():
        result = []

        def add(n, src, dst, where, sends, gets):
            copy = pltpu.make_async_remote_copy(
                src_ref=src, dst_ref=dst, send_sem=face_send.at[n], recv_sem=face_recv.at[n],
                device_id=where, device_id_type=MESH,
            )
            result.append((copy, sends, gets))

        for f, side in ((0, 1), (1, -1)):
            add(f, YS.at[f], YR.at[f], (gx, gy + side, gz), side_y[side], side_y[-side])
        for f, side in ((0, 1), (1, -1)):
            at = TZ - 1 if f == 0 else 0
            where = id_of((side, 0, 0))
            add(2 + f, mi.at[at], HZ.at[f, 0], where, z_ok[side], z_ok[-side])
            add(4 + f, mg.at[:, at], HZ.at[f, pl.ds(1, 3)], where, z_ok[side], z_ok[-side])
            add(6 + f, CT, HC.at[f], where, z_ok[side], z_ok[-side])
        for f, side in ((0, 1), (1, -1)):
            where = id_of((0, side, 0))
            add(8 + f, XS.at[f], HX.at[f], where, x_ok[side], x_ok[-side])
            add(10 + f, CT, HC.at[2 + f], where, x_ok[side], x_ok[-side])
        return result

    def sum_copy(buffer, k, at, where, send, recv):
        return pltpu.make_async_remote_copy(
            src_ref=buffer.at[k, pl.ds(at, 1)], dst_ref=buffer.at[k, pl.ds(at, 1)],
            send_sem=send.at[k], recv_sem=recv.at[k], device_id=where, device_id_type=MESH,
        )

    def sum_all(buffer, k, count, send, recv):
        return pltpu.make_async_remote_copy(
            src_ref=buffer.at[k, pl.ds(0, count)], dst_ref=buffer.at[k, pl.ds(0, count)],
            send_sem=send.at[k], recv_sem=recv.at[k], device_id=plane_peer(1), device_id_type=MESH,
        )

    faces = face_copies()
    for copy, sends, _ in faces[:2]:
        pl.when(sends)(copy.start)
    start(spread_copy, 0)
    for copy, sends, _ in faces[2:]:
        pl.when(sends)(copy.start)

    which = iota((256, 256), 0).astype(F32)

    def picked(rows):
        hit = jnp.zeros((256, rows.shape[1]), F32)
        for k in range(8):
            hit = hit + jnp.where(rows[k : k + 1, :] == which[:, 0 : rows.shape[1]], 1.0, 0.0)
        return hit

    for c in range(3):
        MGS[c, 0:ROWS, :] = mg[c].astype(F32).reshape(ROWS, TY)
    own = picked(CT[...])
    PT2[:, 0:256] = own.astype(BF16)
    PT2[:, 384:640] = own.astype(BF16)
    own_t = own.T.astype(BF16)
    P2[0:256, 0:256] = own_t
    P2[0:256, 256:512] = own_t
    get_tb.wait()
    for c in range(3):
        for n in range(NW):
            TF[c * 16 + n : c * 16 + n + 1, :] = tb[n].astype(F32)[TY - 1 : TY, :]
            TF[c * 16 + 8 + n : c * 16 + 9 + n, :] = tb[n].astype(F32)[0:1, :]
    TF[48:128, :] = jnp.zeros((80, CP), F32)
    TE[...] = TF[...].astype(BF16)
    at_m, at_lane = iota((256, 128), 0), iota((256, 128), 1)
    for i, source in enumerate((
        jnp.where(at_lane < 32, at_lane + 224, -1),
        jnp.where((at_lane >= 32) & (at_lane < 64), at_lane - 32, -1),
        jnp.where((at_lane >= 64) & (at_lane < 72), (at_lane - 64) * TX + TX - 1, -1),
        jnp.where((at_lane >= 72) & (at_lane < 80), (at_lane - 72) * TX, -1),
    )):
        SEL[i] = jnp.where(at_m == source, 1.0, 0.0).astype(BF16)
    get_fg.wait()
    get_vw.wait()
    fixed = [fg[c].astype(F32) for c in range(3)]
    IFS[...] = 1.0 / (fixed[0] * fixed[0] + fixed[1] * fixed[1] + fixed[2] * fixed[2] + EDGE_SQUARED)
    WG[...] = jnp.zeros(WG.shape, BF16)
    for at in (0, 1, 10, 11):
        FZ[at] = jnp.zeros((TX, TY), F32)
    PB[...] = jnp.zeros(PB.shape, F32)

    for copy, _, gets in faces[2:]:
        pl.when(gets)(copy.wait_recv)

    column = iota((1, 128), 1)
    shift = jnp.where(column < 32, -3.0, jnp.where(column < 64, 3.0, jnp.where(column < 72, -1.0, 1.0)))
    rows = None
    for i in range(4):
        part = dot(jnp.concatenate([HC[i], HC[i]], axis=0).astype(BF16), SEL[i])[0:8]
        rows = part if rows is None else rows + part
    halo = picked(rows + shift)
    PT2[:, 256:384] = halo.astype(BF16)
    PT2[:, 640:768] = halo.astype(BF16)
    halo_t = halo.T.astype(BF16)
    P2[256:384, 0:256] = halo_t
    P2[256:384, 256:512] = halo_t
    for c in range(3):
        MGS[c, 256:288, :] = HZ[0, 1 + c].astype(F32)
        MGS[c, 288:320, :] = HZ[1, 1 + c].astype(F32)
        MGS[c, 320:328, :] = HX[0, 8 + c * 8 : 16 + c * 8, :]
        MGS[c, 328:336, :] = HX[1, 8 + c * 8 : 16 + c * 8, :]
    YT[...] = jnp.zeros((128, 256), F32)
    for copy, _, gets in faces[:2]:
        pl.when(gets)(copy.wait_recv)
    for f in range(2):
        for c in range(3):
            YT[c * 16 : c * 16 + 16, :] = jnp.broadcast_to(YR[f, 9 + c : 10 + c, :], (16, 256))
        YT[48:49, :] = YR[f, 8:9, :]
        YC[f] = YT[...].T
        side = picked(YR[f, 0:8, :])
        PYT2[f, :, 0:256] = side.astype(BF16)
        PYT2[f, :, 256:512] = side.astype(BF16)
        side_t = side.T.astype(BF16)
        PY2[f, :, 0:256] = side_t
        PY2[f, :, 256:512] = side_t

    all_blocks(NB, 0, nb_send, nb_recv, True)

    def forward(k):
        near = stacked(jnp.concatenate([NB[k, c, MAIN : MAIN + 32, :] for c in range(3)], axis=0))
        for n in range(NW):
            product = dot_nt(near, tb[n])
            high, low = split(product[0:96] + product[96:192])
            for c in range(3):
                BHL[c, n * 32 : n * 32 + 32, :] = high[c * 32 : c * 32 + 32]
                BHL[c, 256 + n * 32 : 288 + n * 32, :] = low[c * 32 : c * 32 + 32]
        total = None
        for c in range(3):
            part = dot(P2[0:336, :], BHL[c]) * MGS[c]
            total = part if total is None else total + part
        wide_blocks = stacked(jnp.concatenate([NB[k, c] for c in range(3)], axis=0))
        ends = dot_nt(wide_blocks, TE[...])
        ends = ends[0:192] + ends[192:384]
        columns = []
        for f in range(2):
            at = FIRST + 18 * f
            chosen = jnp.zeros((32, 128), F32)
            for c in range(3):
                chosen = jnp.where(lane // 16 == c, ends[c * 64 + at : c * 64 + at + 32], chosen)
            spread = jnp.concatenate(
                [jnp.where(lane % 16 == n + 8 * f, chosen, 0.0) for n in range(NW)], axis=0
            )
            columns.append(jnp.sum(dot(PY2[f], stacked(spread)) * YC[f], axis=1, keepdims=True))
        return total, columns

    total, columns = forward(0)
    WP[1:9] = mi[...].astype(F32) + total[0:256].reshape(TZ, TX, TY)
    for f, at in ((0, 0), (1, 9)):
        WP[at] = HZ[f, 0].astype(F32) + total[256 + 32 * f : 288 + 32 * f]
        WX[f] = HX[f, 0:8, :] + total[320 + 8 * f : 328 + 8 * f]
        WY[f] = jnp.broadcast_to(YC[f, :, 48:49] + columns[f], (256, 128))

    row_at = iota((TX, TY), 0)
    lane_at = iota((TX, TY), 1)

    def backward(k):
        def plane(z, energy):
            here = WP[z + 1]
            rows = pl.ds(pl.multiple_of(z * TX, TX), TX)
            back_x, on_x = pltpu.roll(here, 1, 0), pltpu.roll(here, TX - 1, 0)
            back_x = jnp.where(row_at == 0, WX[0, pl.ds(z, 1), :], back_x)
            on_x = jnp.where(row_at == TX - 1, WX[1, pl.ds(z, 1), :], on_x)
            back_y, on_y = pltpu.roll(here, 1, 1), pltpu.roll(here, TY - 1, 1)
            side = WY[0, rows, :]
            back_y = jnp.where(lane_at == 0, jnp.concatenate([side, side], axis=1), back_y)
            side = WY[1, rows, :]
            on_y = jnp.where(lane_at == TY - 1, jnp.concatenate([side, side], axis=1), on_y)
            grads = (WP[z + 2] - WP[z], on_x - back_x, on_y - back_y)
            fixed = [fg[c, z].astype(F32) for c in range(3)]
            inner = (grads[0] * fixed[0] + grads[1] * fixed[1] + grads[2] * fixed[2]) * 0.5
            moving = (grads[0] * grads[0] + grads[1] * grads[1] + grads[2] * grads[2]) * 0.25 + EDGE_SQUARED
            inverse = 1.0 / moving
            weight = vw[z].astype(F32)
            scaled = weight * inner * IFS[z] * inverse
            term = weight - inner * scaled
            other = 0.5 * scaled * inner * inverse
            flux = [other * grads[c] - scaled * fixed[c] for c in range(3)]
            FZ[z + 2] = flux[0]
            pulled = jnp.where(row_at == 0, 0.0, pltpu.roll(flux[1], 1, 0))
            pulled = pulled - jnp.where(row_at == TX - 1, 0.0, pltpu.roll(flux[1], TX - 1, 0))
            pulled = pulled + jnp.where(lane_at == 0, 0.0, pltpu.roll(flux[2], 1, 1))
            pulled = pulled - jnp.where(lane_at == TY - 1, 0.0, pltpu.roll(flux[2], TY - 1, 1))
            PU[z] = pulled
            PUX[0, pl.ds(z, 1), :] = -flux[1][0:1, :]
            PUX[1, pl.ds(z, 1), :] = flux[1][TX - 1 : TX, :]
            PYB[0, rows, :] = jnp.broadcast_to(-flux[2][:, 0:1], (TX, 128))
            PYB[1, rows, :] = jnp.broadcast_to(flux[2][:, TY - 1 : TY], (TX, 128))
            return energy + term

        energy = lax.fori_loop(0, TZ, plane, jnp.zeros((TX, TY), F32), unroll=UNROLL)
        energy = jnp.sum(energy, axis=0, keepdims=True)
        for f in range(2):
            drawn = jnp.where(lane < 48, PYB[f] * YC[f], 0.0)
            back = dot(PYT2[f], stacked(drawn))
            chosen = jnp.zeros((32, 128), F32)
            for n in range(NW):
                chosen = jnp.where(lane % 16 == n + 8 * f, back[n * 32 : n * 32 + 32], chosen)
            blocks = jnp.concatenate([jnp.where(lane // 16 == c, chosen, 0.0) for c in range(3)], axis=0)
            ends = dot(stacked(blocks), TE[...])
            ends = ends[0:96] + ends[96:192]
            at = FIRST + 18 * f
            for c in range(3):
                PB[k, c, at : at + 32, :] = PB[k, c, at : at + 32, :] + ends[c * 32 : c * 32 + 32]
        start(gather_copy, k, [o for o in NEAR if abs(o[2]) == 2])

        def put(block, rows, at):
            for c in range(3):
                high, low = split(block * MGS[c, pl.ds(at, rows), :])
                WG[c, pl.ds(at, rows), :] = high
                WG[c, pl.ds(at + 384, rows), :] = low

        def weigh(z, carry):
            put(PU[z] + FZ[z + 1] - FZ[z + 3], TX, pl.multiple_of(z * TX, TX))
            return carry

        lax.fori_loop(0, TZ, weigh, 0, unroll=UNROLL)
        put(-FZ[2], TX, 256)
        put(FZ[9], TX, 288)
        put(jnp.concatenate([PUX[0], PUX[1]], axis=0), 16, 320)
        for c in range(3):
            high, low = split(dot(PT2[...], WG[c]))
            for n in range(NW):
                GS[c * 32 : c * 32 + 32, n * 256 : n * 256 + 256] = high[n * 32 : n * 32 + 32]
                GS[96 + c * 32 : 128 + c * 32, n * 256 : n * 256 + 256] = low[n * 32 : n * 32 + 32]
        partial = dot(GS[...], tb[...].reshape(NW * TY, CP))
        partial = partial[0:96] + partial[96:192]
        for c in range(3):
            PB[k, c, MAIN : MAIN + 27, :] = PB[k, c, MAIN : MAIN + 27, :] + partial[c * 32 : c * 32 + 27]
        return energy[:, 0:128] + energy[:, 128:256]

    def reduce_gradient(k, energy):
        start(gather_copy, k, REST)
        for c in range(3):
            RB[k, c, CENTRE : CENTRE + 1, :] = PB[k, c, CENTRE : CENTRE + 1, :]
        all_blocks(RB, k, rb_send, rb_recv, True)
        gradient = [jnp.sum(RB[k, c], axis=0, keepdims=True) for c in range(3)]
        square = gradient[0] * gradient[0] + gradient[1] * gradient[1] + gradient[2] * gradient[2]
        energy = energy + pltpu.roll(energy, 64, 1)
        square = square + pltpu.roll(square, 64, 1)
        AP[k, pl.ds(plane_at, 1), :] = jnp.where(lane < 64, energy, square)
        for r in PLANE:
            sum_copy(AP, k, plane_at, plane_peer(r), ap_send, ap_recv).start()
        return gradient

    def pass_on(k):
        sum_all(AP, k, 31, ap_send, ap_recv).wait_recv()
        AZ[k, pl.ds(ring_at, 1), :] = jnp.sum(AP[k], axis=0, keepdims=True)
        for r in RING:
            sum_copy(AZ, k, ring_at, ring_peer(r), az_send, az_recv).start()

    def take_sum(k):
        sum_all(AZ, k, 15, az_send, az_recv).wait_recv()
        sums = jnp.sum(AZ[k], axis=0, keepdims=True)
        energy = jnp.sum(jnp.where(lane < 64, sums, 0.0), axis=1, keepdims=True)
        square = jnp.sum(jnp.where(lane < 64, 0.0, sums), axis=1, keepdims=True)
        devices = NX * NY * NZ
        step_size = STEP_LENGTH * lax.rsqrt(square * (1.0 / (devices * 3 * CP)) + 1e-06)
        return energy * (1.0 / (devices * TZ * TX * TY)), step_size

    energy = backward(0)
    first = reduce_gradient(0, energy)
    for c in range(3):
        NB[1, c, CENTRE : CENTRE + 1, :] = first[c]
    start(spread_copy, 1)
    pass_on(0)
    for copy, sends, _ in faces:
        pl.when(sends)(copy.wait_send)
    all_blocks(NB, 0, nb_send, nb_recv, False)
    all_blocks(NB, 1, nb_send, nb_recv, True)
    total, columns = forward(1)
    energy_0, size_0 = take_sum(0)
    WP[1:9] = WP[1:9] - size_0[0, 0] * total[0:256].reshape(TZ, TX, TY)
    for f, at in ((0, 0), (1, 9)):
        WP[at] = WP[at] - size_0 * total[256 + 32 * f : 288 + 32 * f]
        WX[f] = WX[f] - size_0 * total[320 + 8 * f : 328 + 8 * f]
        WY[f] = WY[f] - size_0 * columns[f]
    out_w[...] = WP[1:9]
    energy = backward(1)
    second = reduce_gradient(1, energy)
    all_blocks(RB, 0, rb_send, rb_recv, False)
    all_blocks(NB, 1, nb_send, nb_recv, False)
    sum_all(AP, 0, 31, ap_send, ap_recv).wait_send()
    sum_all(AZ, 0, 15, az_send, az_recv).wait_send()
    pass_on(1)
    all_blocks(RB, 1, rb_send, rb_recv, False)
    sum_all(AP, 1, 31, ap_send, ap_recv).wait_send()
    energy_1, size_1 = take_sum(1)
    sum_all(AZ, 1, 15, az_send, az_recv).wait_send()
    for c in range(3):
        out_c[c] = NB[0, c, CENTRE : CENTRE + 1, :] - size_0 * first[c] - size_1 * second[c]
    out_e[0] = energy_0[0, 0]
    out_e[1] = energy_1[0, 0]


def hand_over(new, warped, energies, out_c, out_w, out_e, done):
    copies = [
        pltpu.make_async_copy(src, dst, done.at[n])
        for n, (src, dst) in enumerate(((warped, out_w), (new, out_c), (energies, out_e)))
    ]
    for copy in copies:
        copy.start()
    for copy in copies:
        copy.wait()


def on_device(moving_image, moving_grad, fixed_grad, voxel_weight, coefficients, weight_table, ctrl_slot, weight_slot):
    whole = pl.BlockSpec(memory_space=pltpu.VMEM)
    vmem = pltpu.VMEM
    sem = pltpu.SemaphoreType.DMA
    new, warped, energies = pl.pallas_call(
        kernel,
        out_shape=(
            jax.ShapeDtypeStruct((3, 1, CP), F32),
            jax.ShapeDtypeStruct((TZ, TX, TY), F32),
            jax.ShapeDtypeStruct((2,), F32),
        ),
        in_specs=[pl.BlockSpec(memory_space=pltpu.HBM)] * 8,
        out_specs=(whole, whole, pl.BlockSpec(memory_space=pltpu.SMEM)),
        scratch_shapes=[
            vmem((TZ, TX, TY), BF16),
            vmem((3, TZ, TX, TY), BF16),
            vmem((3, TZ, TX, TY), BF16),
            vmem((TZ, TX, TY), BF16),
            vmem((NW, TY, CP), BF16),
            vmem((8, ROWS), jnp.int32),
            vmem((8, ROWS), jnp.int32),
            vmem((2, 3, 64, CP), F32),
            vmem((2, 3, 64, CP), F32),
            vmem((2, 3, 64, CP), F32),
            vmem((2, 32, 128), F32),
            vmem((2, 16, 128), F32),
            vmem((8, ROWS), F32),
            vmem((4, 8, ROWS), F32),
            vmem((4, ROWS, 128), BF16),
            vmem((2, 4, TX, TY), BF16),
            vmem((2, 32, TY), F32),
            vmem((2, 32, TY), F32),
            vmem((2, 16, TY), F32),
            vmem((2, 16, TY), F32),
            vmem((384, 512), BF16),
            vmem((256, 768), BF16),
            vmem((2, 256, 512), BF16),
            vmem((2, 256, 512), BF16),
            vmem((3, 336, TY), F32),
            vmem((2, 256, 128), F32),
            vmem((3, 512, TY), BF16),
            vmem((10, TX, TY), F32),
            vmem((2, 8, TY), F32),
            vmem((2, 256, 128), F32),
            vmem((TZ, TX, TY), F32),
            vmem((12, TX, TY), F32),
            vmem((TZ, TX, TY), F32),
            vmem((2, 8, TY), F32),
            vmem((2, 256, 128), F32),
            vmem((3, 768, TY), BF16),
            vmem((192, 2048), BF16),
            vmem((128, CP), F32),
            vmem((128, CP), BF16),
            vmem((128, 256), F32),
            sem((8,)), sem((2,)), sem((2,)), sem((2,)), sem((2,)),
            sem((12,)), sem((12,)), sem((2,)), sem((2,)), sem((2,)), sem((2,)),
        ],
        compiler_params=pltpu.CompilerParams(
            collective_id=0, has_side_effects=True, vmem_limit_bytes=63 * 1024 * 1024
        ),
    )(
        moving_image, moving_grad, fixed_grad, voxel_weight, coefficients.reshape(3, 1, CP), weight_table,
        ctrl_slot.reshape(ROWS, 8).T, weight_slot.reshape(ROWS, 8).T,
    )
    hbm = pl.BlockSpec(memory_space=pltpu.HBM)
    new, warped, energies = pl.pallas_call(
        hand_over,
        out_shape=(
            jax.ShapeDtypeStruct((3, 1, CP), F32),
            jax.ShapeDtypeStruct((TZ, TX, TY), F32),
            jax.ShapeDtypeStruct((2,), F32),
        ),
        in_specs=[whole, whole, pl.BlockSpec(memory_space=pltpu.SMEM)],
        out_specs=(hbm, hbm, hbm),
        scratch_shapes=[sem((3,))],
    )(new, warped, energies)
    return new.reshape(1, 1, 1, 3, CP), warped, energies


def solution(mesh):
    in_specs = (
        P("gz", "gx", "gy"),
        P(None, "gz", "gx", "gy"),
        P(None, "gz", "gx", "gy"),
        P("gz", "gx", "gy"),
        P("gz", "gx", "gy", None, None),
        P(),
        P("gz", "gx", "gy", None, None),
        P("gz", "gx", "gy", None, None),
    )
    out_specs = (P("gz", "gx", "gy", None, None), P("gz", "gx", "gy"), P())
    return jax.shard_map(on_device, mesh=mesh, in_specs=in_specs, out_specs=out_specs, check_vma=False)
```

```python
import functools

import jax
import jax.numpy as jnp
from jax import lax
from jax.experimental import pallas as pl
from jax.experimental.pallas import tpu as pltpu
from jax.sharding import PartitionSpec as P

MESH = pl.DeviceIdType.MESH
F32 = jnp.float32
BF16 = jnp.bfloat16
EDGE_SQUARED = 0.05
STEP_LENGTH = 0.05
NX, NY, NZ = 4, 16, 8
TZ, TX, TY, CP, NW = 8, 32, 256, 128, 8
ROWS = TZ * TX
FIRST = 7
CENTRE = FIRST + 22
MAIN = FIRST + 9
UNROLL = 8


def split(x):
    high = x.astype(BF16)
    return high, (x - high.astype(F32)).astype(BF16)


def stacked(x):
    return jnp.concatenate(split(x), axis=0)


def dot(a, b):
    return jnp.dot(a, b, preferred_element_type=F32)


def dot_nt(a, b):
    return lax.dot_general(a, b, (((1,), (1,)), ((), ())), preferred_element_type=F32)


def iota(shape, dim):
    return lax.broadcasted_iota(jnp.int32, shape, dim)


NEAR = [
    (dz, dx, dy) for dy in (2, 1, -2, -1, 0) for dx in (-1, 1, 0) for dz in (0, -1, 1) if (dz, dx, dy) != (0, 0, 0)
]
REST = [o for o in NEAR if abs(o[2]) < 2]
PLANE = sorted(
    range(1, 32), key=lambda r: -(min(r // 8, 4 - r // 8) + min(r % 8 // 2, 4 - r % 8 // 2))
)
RING = (8, 7, 9, 6, 10, 5, 11, 4, 12, 3, 13, 2, 14, 1, 15)
COUNTS = sorted({a * b * c - 1 for a in (2, 3) for b in (2, 3) for c in (3, 4, 5)})


def kernel(
    mi_in, mg_in, fg_in, vw_in, co_in, tb_in, cs_in, ws_in,
    out_c, out_w, out_e,
    mi, mg, fg, vw, tb, cs, ws,
    NB, PB, RB, AP, AZ, CT, HC, SEL, HZ, HX, XS, YS, YR, P2, PT2, PY2, PYT2, MGS, YC, BHL,
    WP, WX, WY, IFS, FZ, PU, PUX, PYB, WG, GS, TF, TE, YT,
    in_sem, nb_send, nb_recv, rb_send, rb_recv, face_send, face_recv, ap_send, ap_recv, az_send, az_recv,
):
    gx, gy, gz = lax.axis_index("gx"), lax.axis_index("gy"), lax.axis_index("gz")
    lane = iota((1, 128), 1)
    plane_at = gx * 8 + gy % 8
    ring_at = (gy // 8) * 8 + gz

    mine = (gx, gy, gz)

    def plane_peer(r):
        other = (plane_at + r) % 32
        return (other // 8, (gy // 8) * 8 + other % 8, gz)

    def ring_peer(r):
        other = (ring_at + r) % 16
        return (gx, (other // 8) * 8 + gy % 8, other % 8)

    z_ok = {-1: gz > 0, 0: None, 1: gz < NZ - 1}
    x_ok = {-1: gx > 0, 0: None, 1: gx < NX - 1}
    side_y = {-1: gy > 0, 1: gy < NY - 1}
    toward = 1 - 2 * (gy // (NY // 2))
    out = jnp.where(gy < NY // 2, gy, NY - 1 - gy)
    y_ok = {-2: out > 1, -1: out > 0, 0: None, 1: None, 2: None}

    def both(a, b):
        return b if a is None else a if b is None else a & b

    flat_ok = {(dz, dx): both(z_ok[dz], x_ok[dx]) for dz in z_ok for dx in x_ok}

    def there(o):
        found = both(flat_ok[o[0], o[1]], y_ok[o[2]])
        return gx >= 0 if found is None else found

    def id_of(o):
        return (gx + o[1], gy + toward * o[2], gz + o[0])

    def index_of(o):
        return (toward * o[2] + 2) * 9 + ((o[0] + 1) * 3 + o[1] + 1)

    def fetch(n, src, dst):
        copy = pltpu.make_async_copy(src, dst, in_sem.at[n])
        copy.start()
        return copy

    for ref in (NB, RB, HC, HZ, HX, YR):
        ref[...] = jnp.zeros(ref.shape, ref.dtype)
    get_co = fetch(0, co_in, NB.at[0, :, pl.ds(CENTRE, 1), :])
    get_cs = fetch(1, cs_in, cs)
    get_ws = fetch(2, ws_in, ws)
    get_mi = fetch(3, mi_in, mi)
    get_mg = fetch(4, mg_in, mg)
    get_tb = fetch(5, tb_in, tb)
    get_fg = fetch(6, fg_in, fg)
    get_vw = fetch(7, vw_in, vw)

    barrier = pltpu.get_barrier_semaphore()

    def greet(where):
        pl.semaphore_signal(barrier, inc=1, device_id=where, device_id_type=MESH)

    for o in NEAR[:36]:
        pl.when(there(o))(functools.partial(greet, id_of(o)))
    for r in RING:
        greet(ring_peer(r))
    for r in PLANE:
        greet(plane_peer(r))
    for o in NEAR[36:]:
        pl.when(there(o))(functools.partial(greet, id_of(o)))

    get_cs.wait()
    get_ws.wait()
    slot = cs[...]
    third = (slot * 11) >> 5
    comb = (ws[...] * 32 + (slot - 3 * third) * 9 + third).astype(F32)
    CT[...] = comb
    YS[0, 0:8, :] = comb
    YS[1, 0:8, :] = comb
    YS[:, 8:16, :] = jnp.zeros((2, 8, TY), F32)
    get_mi.wait()
    get_mg.wait()
    ends_at = iota((16, TY), 0)
    ends = jnp.where(iota((16, TY), 1) == jnp.where(ends_at == 0, TY - 1, 0), jnp.where(ends_at < 2, 1.0, 0.0), 0.0)
    ends = ends.astype(BF16)
    for a in range(4):
        rows = dot_nt(ends, (mi[...] if a == 0 else mg[a - 1]).reshape(ROWS, TY))
        YS[0, 8 + a : 9 + a, :] = rows[0:1]
        YS[1, 8 + a : 9 + a, :] = rows[1:2]
    for a in range(4):
        for z in range(TZ):
            whole = mi[z] if a == 0 else mg[a - 1, z]
            XS[0, a * 8 + z : a * 8 + z + 1, :] = whole.astype(F32)[TX - 1 : TX, :]
            XS[1, a * 8 + z : a * 8 + z + 1, :] = whole.astype(F32)[0:1, :]

    count_z = 3 - (gz == 0).astype(jnp.int32) - (gz == NZ - 1).astype(jnp.int32)
    count_x = 3 - (gx == 0).astype(jnp.int32) - (gx == NX - 1).astype(jnp.int32)
    count_y = jnp.minimum(gy, 2) + jnp.minimum(NY - 1 - gy, 2) + 1
    near_count = count_z * count_x * count_y - 1
    get_co.wait()
    pl.semaphore_wait(barrier, near_count + 46)

    def block_copy(buffer_from, row_from, buffer_to, row_to, send, recv, where):
        return pltpu.make_async_remote_copy(
            src_ref=buffer_from.at[:, pl.ds(row_from, 1), :],
            dst_ref=buffer_to.at[:, pl.ds(row_to, 1), :],
            send_sem=send, recv_sem=recv, device_id=where, device_id_type=MESH,
        )

    def spread_copy(k, o):
        u = index_of(o)
        return block_copy(NB.at[k], CENTRE, NB.at[k], FIRST + 44 - u, nb_send.at[k], nb_recv.at[k], id_of(o))

    def gather_copy(k, o):
        u = index_of(o)
        return block_copy(PB.at[k], FIRST + u, RB.at[k], FIRST + 44 - u, rb_send.at[k], rb_recv.at[k], id_of(o))

    def start(maker, k, offsets=NEAR):
        for o in offsets:
            pl.when(there(o))(maker(k, o).start)

    def all_blocks(buffer, k, send, recv, receive):
        for count in COUNTS:
            blocks = buffer.at[k, :, pl.ds(0, count), :]
            copy = pltpu.make_async_remote_copy(
                src_ref=blocks, dst_ref=blocks, send_sem=send.at[k], recv_sem=recv.at[k],
                device_id=mine, device_id_type=MESH,
            )
            pl.when(near_count == count)(copy.wait_recv if receive else copy.wait_send)

    def face_copies():
        result = []

        def add(n, src, dst, where, sends, gets):
            copy = pltpu.make_async_remote_copy(
                src_ref=src, dst_ref=dst, send_sem=face_send.at[n], recv_sem=face_recv.at[n],
                device_id=where, device_id_type=MESH,
            )
            result.append((copy, sends, gets))

        for f, side in ((0, 1), (1, -1)):
            add(f, YS.at[f], YR.at[f], (gx, gy + side, gz), side_y[side], side_y[-side])
        for f, side in ((0, 1), (1, -1)):
            at = TZ - 1 if f == 0 else 0
            where = id_of((side, 0, 0))
            add(2 + f, mi.at[at], HZ.at[f, 0], where, z_ok[side], z_ok[-side])
            add(4 + f, mg.at[:, at], HZ.at[f, pl.ds(1, 3)], where, z_ok[side], z_ok[-side])
            add(6 + f, CT, HC.at[f], where, z_ok[side], z_ok[-side])
        for f, side in ((0, 1), (1, -1)):
            where = id_of((0, side, 0))
            add(8 + f, XS.at[f], HX.at[f], where, x_ok[side], x_ok[-side])
            add(10 + f, CT, HC.at[2 + f], where, x_ok[side], x_ok[-side])
        return result

    def sum_copy(buffer, k, at, where, send, recv):
        return pltpu.make_async_remote_copy(
            src_ref=buffer.at[k, pl.ds(at, 1)], dst_ref=buffer.at[k, pl.ds(at, 1)],
            send_sem=send.at[k], recv_sem=recv.at[k], device_id=where, device_id_type=MESH,
        )

    def sum_all(buffer, k, count, send, recv):
        return pltpu.make_async_remote_copy(
            src_ref=buffer.at[k, pl.ds(0, count)], dst_ref=buffer.at[k, pl.ds(0, count)],
            send_sem=send.at[k], recv_sem=recv.at[k], device_id=plane_peer(1), device_id_type=MESH,
        )

    faces = face_copies()
    for copy, sends, _ in faces[:2]:
        pl.when(sends)(copy.start)
    start(spread_copy, 0)
    for copy, sends, _ in faces[2:]:
        pl.when(sends)(copy.start)

    which = iota((256, 256), 0).astype(F32)

    def picked(rows):
        hit = jnp.zeros((256, rows.shape[1]), F32)
        for k in range(8):
            hit = hit + jnp.where(rows[k : k + 1, :] == which[:, 0 : rows.shape[1]], 1.0, 0.0)
        return hit

    for c in range(3):
        MGS[c, 0:ROWS, :] = mg[c].astype(F32).reshape(ROWS, TY)
    own = picked(CT[...])
    PT2[:, 0:256] = own.astype(BF16)
    PT2[:, 384:640] = own.astype(BF16)
    own_t = own.T.astype(BF16)
    P2[0:256, 0:256] = own_t
    P2[0:256, 256:512] = own_t
    get_tb.wait()
    for c in range(3):
        for n in range(NW):
            TF[c * 16 + n : c * 16 + n + 1, :] = tb[n].astype(F32)[TY - 1 : TY, :]
            TF[c * 16 + 8 + n : c * 16 + 9 + n, :] = tb[n].astype(F32)[0:1, :]
    TF[48:128, :] = jnp.zeros((80, CP), F32)
    TE[...] = TF[...].astype(BF16)
    at_m, at_lane = iota((256, 128), 0), iota((256, 128), 1)
    for i, source in enumerate((
        jnp.where(at_lane < 32, at_lane + 224, -1),
        jnp.where((at_lane >= 32) & (at_lane < 64), at_lane - 32, -1),
        jnp.where((at_lane >= 64) & (at_lane < 72), (at_lane - 64) * TX + TX - 1, -1),
        jnp.where((at_lane >= 72) & (at_lane < 80), (at_lane - 72) * TX, -1),
    )):
        SEL[i] = jnp.where(at_m == source, 1.0, 0.0).astype(BF16)
    get_fg.wait()
    get_vw.wait()
    fixed = [fg[c].astype(F32) for c in range(3)]
    IFS[...] = 1.0 / (fixed[0] * fixed[0] + fixed[1] * fixed[1] + fixed[2] * fixed[2] + EDGE_SQUARED)
    WG[...] = jnp.zeros(WG.shape, BF16)
    for at in (0, 1, 10, 11):
        FZ[at] = jnp.zeros((TX, TY), F32)
    PB[...] = jnp.zeros(PB.shape, F32)

    for copy, _, gets in faces[2:]:
        pl.when(gets)(copy.wait_recv)

    column = iota((1, 128), 1)
    shift = jnp.where(column < 32, -3.0, jnp.where(column < 64, 3.0, jnp.where(column < 72, -1.0, 1.0)))
    rows = None
    for i in range(4):
        part = dot(jnp.concatenate([HC[i], HC[i]], axis=0).astype(BF16), SEL[i])[0:8]
        rows = part if rows is None else rows + part
    halo = picked(rows + shift)
    PT2[:, 256:384] = halo.astype(BF16)
    PT2[:, 640:768] = halo.astype(BF16)
    halo_t = halo.T.astype(BF16)
    P2[256:384, 0:256] = halo_t
    P2[256:384, 256:512] = halo_t
    for c in range(3):
        MGS[c, 256:288, :] = HZ[0, 1 + c].astype(F32)
        MGS[c, 288:320, :] = HZ[1, 1 + c].astype(F32)
        MGS[c, 320:328, :] = HX[0, 8 + c * 8 : 16 + c * 8, :]
        MGS[c, 328:336, :] = HX[1, 8 + c * 8 : 16 + c * 8, :]
    YT[...] = jnp.zeros((128, 256), F32)
    for copy, _, gets in faces[:2]:
        pl.when(gets)(copy.wait_recv)
    for f in range(2):
        for c in range(3):
            YT[c * 16 : c * 16 + 16, :] = jnp.broadcast_to(YR[f, 9 + c : 10 + c, :], (16, 256))
        YT[48:49, :] = YR[f, 8:9, :]
        YC[f] = YT[...].T
        side = picked(YR[f, 0:8, :])
        PYT2[f, :, 0:256] = side.astype(BF16)
        PYT2[f, :, 256:512] = side.astype(BF16)
        side_t = side.T.astype(BF16)
        PY2[f, :, 0:256] = side_t
        PY2[f, :, 256:512] = side_t

    all_blocks(NB, 0, nb_send, nb_recv, True)

    def forward(k):
        near = stacked(jnp.concatenate([NB[k, c, MAIN : MAIN + 32, :] for c in range(3)], axis=0))
        for n in range(NW):
            product = dot_nt(near, tb[n])
            high, low = split(product[0:96] + product[96:192])
            for c in range(3):
                BHL[c, n * 32 : n * 32 + 32, :] = high[c * 32 : c * 32 + 32]
                BHL[c, 256 + n * 32 : 288 + n * 32, :] = low[c * 32 : c * 32 + 32]
        total = None
        for c in range(3):
            part = dot(P2[0:336, :], BHL[c]) * MGS[c]
            total = part if total is None else total + part
        wide_blocks = stacked(jnp.concatenate([NB[k, c] for c in range(3)], axis=0))
        ends = dot_nt(wide_blocks, TE[...])
        ends = ends[0:192] + ends[192:384]
        columns = []
        for f in range(2):
            at = FIRST + 18 * f
            chosen = jnp.zeros((32, 128), F32)
            for c in range(3):
                chosen = jnp.where(lane // 16 == c, ends[c * 64 + at : c * 64 + at + 32], chosen)
            spread = jnp.concatenate(
                [jnp.where(lane % 16 == n + 8 * f, chosen, 0.0) for n in range(NW)], axis=0
            )
            columns.append(jnp.sum(dot(PY2[f], stacked(spread)) * YC[f], axis=1, keepdims=True))
        return total, columns

    total, columns = forward(0)
    WP[1:9] = mi[...].astype(F32) + total[0:256].reshape(TZ, TX, TY)
    for f, at in ((0, 0), (1, 9)):
        WP[at] = HZ[f, 0].astype(F32) + total[256 + 32 * f : 288 + 32 * f]
        WX[f] = HX[f, 0:8, :] + total[320 + 8 * f : 328 + 8 * f]
        WY[f] = jnp.broadcast_to(YC[f, :, 48:49] + columns[f], (256, 128))

    row_at = iota((TX, TY), 0)
    lane_at = iota((TX, TY), 1)

    def backward(k):
        def plane(z, energy):
            here = WP[z + 1]
            rows = pl.ds(pl.multiple_of(z * TX, TX), TX)
            back_x, on_x = pltpu.roll(here, 1, 0), pltpu.roll(here, TX - 1, 0)
            back_x = jnp.where(row_at == 0, WX[0, pl.ds(z, 1), :], back_x)
            on_x = jnp.where(row_at == TX - 1, WX[1, pl.ds(z, 1), :], on_x)
            back_y, on_y = pltpu.roll(here, 1, 1), pltpu.roll(here, TY - 1, 1)
            side = WY[0, rows, :]
            back_y = jnp.where(lane_at == 0, jnp.concatenate([side, side], axis=1), back_y)
            side = WY[1, rows, :]
            on_y = jnp.where(lane_at == TY - 1, jnp.concatenate([side, side], axis=1), on_y)
            grads = (WP[z + 2] - WP[z], on_x - back_x, on_y - back_y)
            fixed = [fg[c, z].astype(F32) for c in range(3)]
            inner = (grads[0] * fixed[0] + grads[1] * fixed[1] + grads[2] * fixed[2]) * 0.5
            moving = (grads[0] * grads[0] + grads[1] * grads[1] + grads[2] * grads[2]) * 0.25 + EDGE_SQUARED
            inverse = 1.0 / moving
            weight = vw[z].astype(F32)
            scaled = weight * inner * IFS[z] * inverse
            term = weight - inner * scaled
            other = 0.5 * scaled * inner * inverse
            flux = [other * grads[c] - scaled * fixed[c] for c in range(3)]
            FZ[z + 2] = flux[0]
            pulled = jnp.where(row_at == 0, 0.0, pltpu.roll(flux[1], 1, 0))
            pulled = pulled - jnp.where(row_at == TX - 1, 0.0, pltpu.roll(flux[1], TX - 1, 0))
            pulled = pulled + jnp.where(lane_at == 0, 0.0, pltpu.roll(flux[2], 1, 1))
            pulled = pulled - jnp.where(lane_at == TY - 1, 0.0, pltpu.roll(flux[2], TY - 1, 1))
            PU[z] = pulled
            PUX[0, pl.ds(z, 1), :] = -flux[1][0:1, :]
            PUX[1, pl.ds(z, 1), :] = flux[1][TX - 1 : TX, :]
            PYB[0, rows, :] = jnp.broadcast_to(-flux[2][:, 0:1], (TX, 128))
            PYB[1, rows, :] = jnp.broadcast_to(flux[2][:, TY - 1 : TY], (TX, 128))
            return energy + term

        energy = lax.fori_loop(0, TZ, plane, jnp.zeros((TX, TY), F32), unroll=UNROLL)
        energy = jnp.sum(energy, axis=0, keepdims=True)
        for f in range(2):
            drawn = jnp.where(lane < 48, PYB[f] * YC[f], 0.0)
            back = dot(PYT2[f], stacked(drawn))
            chosen = jnp.zeros((32, 128), F32)
            for n in range(NW):
                chosen = jnp.where(lane % 16 == n + 8 * f, back[n * 32 : n * 32 + 32], chosen)
            blocks = jnp.concatenate([jnp.where(lane // 16 == c, chosen, 0.0) for c in range(3)], axis=0)
            ends = dot(stacked(blocks), TE[...])
            ends = ends[0:96] + ends[96:192]
            at = FIRST + 18 * f
            for c in range(3):
                PB[k, c, at : at + 32, :] = PB[k, c, at : at + 32, :] + ends[c * 32 : c * 32 + 32]
        start(gather_copy, k, [o for o in NEAR if abs(o[2]) == 2])

        def put(block, rows, at):
            for c in range(3):
                high, low = split(block * MGS[c, pl.ds(at, rows), :])
                WG[c, pl.ds(at, rows), :] = high
                WG[c, pl.ds(at + 384, rows), :] = low

        def weigh(z, carry):
            put(PU[z] + FZ[z + 1] - FZ[z + 3], TX, pl.multiple_of(z * TX, TX))
            return carry

        lax.fori_loop(0, TZ, weigh, 0, unroll=UNROLL)
        put(-FZ[2], TX, 256)
        put(FZ[9], TX, 288)
        put(jnp.concatenate([PUX[0], PUX[1]], axis=0), 16, 320)
        for c in range(3):
            high, low = split(dot(PT2[...], WG[c]))
            for n in range(NW):
                GS[c * 32 : c * 32 + 32, n * 256 : n * 256 + 256] = high[n * 32 : n * 32 + 32]
                GS[96 + c * 32 : 128 + c * 32, n * 256 : n * 256 + 256] = low[n * 32 : n * 32 + 32]
        partial = dot(GS[...], tb[...].reshape(NW * TY, CP))
        partial = partial[0:96] + partial[96:192]
        for c in range(3):
            PB[k, c, MAIN : MAIN + 27, :] = PB[k, c, MAIN : MAIN + 27, :] + partial[c * 32 : c * 32 + 27]
        return energy[:, 0:128] + energy[:, 128:256]

    def reduce_gradient(k, energy):
        start(gather_copy, k, REST)
        for c in range(3):
            RB[k, c, CENTRE : CENTRE + 1, :] = PB[k, c, CENTRE : CENTRE + 1, :]
        all_blocks(RB, k, rb_send, rb_recv, True)
        gradient = [jnp.sum(RB[k, c], axis=0, keepdims=True) for c in range(3)]
        square = gradient[0] * gradient[0] + gradient[1] * gradient[1] + gradient[2] * gradient[2]
        energy = energy + pltpu.roll(energy, 64, 1)
        square = square + pltpu.roll(square, 64, 1)
        AP[k, pl.ds(plane_at, 1), :] = jnp.where(lane < 64, energy, square)
        for r in PLANE:
            sum_copy(AP, k, plane_at, plane_peer(r), ap_send, ap_recv).start()
        return gradient

    def pass_on(k):
        sum_all(AP, k, 31, ap_send, ap_recv).wait_recv()
        AZ[k, pl.ds(ring_at, 1), :] = jnp.sum(AP[k], axis=0, keepdims=True)
        for r in RING:
            sum_copy(AZ, k, ring_at, ring_peer(r), az_send, az_recv).start()

    def take_sum(k):
        sum_all(AZ, k, 15, az_send, az_recv).wait_recv()
        sums = jnp.sum(AZ[k], axis=0, keepdims=True)
        energy = jnp.sum(jnp.where(lane < 64, sums, 0.0), axis=1, keepdims=True)
        square = jnp.sum(jnp.where(lane < 64, 0.0, sums), axis=1, keepdims=True)
        devices = NX * NY * NZ
        step_size = STEP_LENGTH * lax.rsqrt(square * (1.0 / (devices * 3 * CP)) + 1e-06)
        return energy * (1.0 / (devices * TZ * TX * TY)), step_size

    energy = backward(0)
    first = reduce_gradient(0, energy)
    for c in range(3):
        NB[1, c, CENTRE : CENTRE + 1, :] = first[c]
    start(spread_copy, 1)
    pass_on(0)
    for copy, sends, _ in faces:
        pl.when(sends)(copy.wait_send)
    all_blocks(NB, 0, nb_send, nb_recv, False)
    all_blocks(NB, 1, nb_send, nb_recv, True)
    total, columns = forward(1)
    energy_0, size_0 = take_sum(0)
    WP[1:9] = WP[1:9] - size_0[0, 0] * total[0:256].reshape(TZ, TX, TY)
    for f, at in ((0, 0), (1, 9)):
        WP[at] = WP[at] - size_0 * total[256 + 32 * f : 288 + 32 * f]
        WX[f] = WX[f] - size_0 * total[320 + 8 * f : 328 + 8 * f]
        WY[f] = WY[f] - size_0 * columns[f]
    put_w = pltpu.make_async_copy(WP.at[pl.ds(1, TZ)], out_w, in_sem.at[0])
    put_w.start()
    energy = backward(1)
    second = reduce_gradient(1, energy)
    all_blocks(RB, 0, rb_send, rb_recv, False)
    all_blocks(NB, 1, nb_send, nb_recv, False)
    sum_all(AP, 0, 31, ap_send, ap_recv).wait_send()
    sum_all(AZ, 0, 15, az_send, az_recv).wait_send()
    pass_on(1)
    all_blocks(RB, 1, rb_send, rb_recv, False)
    sum_all(AP, 1, 31, ap_send, ap_recv).wait_send()
    energy_1, size_1 = take_sum(1)
    sum_all(AZ, 1, 15, az_send, az_recv).wait_send()
    put_w.wait()
    for c in range(3):
        out_c[c] = NB[0, c, CENTRE : CENTRE + 1, :] - size_0 * first[c] - size_1 * second[c]
    out_e[0] = energy_0[0, 0]
    out_e[1] = energy_1[0, 0]


def hand_over(new, warped, energies, out_c, out_w, out_e, done):
    copies = [
        pltpu.make_async_copy(src, dst, done.at[n])
        for n, (src, dst) in enumerate(((warped, out_w), (new, out_c), (energies, out_e)))
    ]
    for copy in copies:
        copy.start()
    for copy in copies:
        copy.wait()


def on_device(moving_image, moving_grad, fixed_grad, voxel_weight, coefficients, weight_table, ctrl_slot, weight_slot):
    whole = pl.BlockSpec(memory_space=pltpu.VMEM)
    vmem = pltpu.VMEM
    sem = pltpu.SemaphoreType.DMA
    new, warped, energies = pl.pallas_call(
        kernel,
        out_shape=(
            jax.ShapeDtypeStruct((3, 1, CP), F32),
            jax.ShapeDtypeStruct((TZ, TX, TY), F32),
            jax.ShapeDtypeStruct((2,), F32),
        ),
        in_specs=[pl.BlockSpec(memory_space=pltpu.HBM)] * 8,
        out_specs=(whole, pl.BlockSpec(memory_space=pltpu.HBM), pl.BlockSpec(memory_space=pltpu.SMEM)),
        scratch_shapes=[
            vmem((TZ, TX, TY), BF16),
            vmem((3, TZ, TX, TY), BF16),
            vmem((3, TZ, TX, TY), BF16),
            vmem((TZ, TX, TY), BF16),
            vmem((NW, TY, CP), BF16),
            vmem((8, ROWS), jnp.int32),
            vmem((8, ROWS), jnp.int32),
            vmem((2, 3, 64, CP), F32),
            vmem((2, 3, 64, CP), F32),
            vmem((2, 3, 64, CP), F32),
            vmem((2, 32, 128), F32),
            vmem((2, 16, 128), F32),
            vmem((8, ROWS), F32),
            vmem((4, 8, ROWS), F32),
            vmem((4, ROWS, 128), BF16),
            vmem((2, 4, TX, TY), BF16),
            vmem((2, 32, TY), F32),
            vmem((2, 32, TY), F32),
            vmem((2, 16, TY), F32),
            vmem((2, 16, TY), F32),
            vmem((384, 512), BF16),
            vmem((256, 768), BF16),
            vmem((2, 256, 512), BF16),
            vmem((2, 256, 512), BF16),
            vmem((3, 336, TY), F32),
            vmem((2, 256, 128), F32),
            vmem((3, 512, TY), BF16),
            vmem((10, TX, TY), F32),
            vmem((2, 8, TY), F32),
            vmem((2, 256, 128), F32),
            vmem((TZ, TX, TY), F32),
            vmem((12, TX, TY), F32),
            vmem((TZ, TX, TY), F32),
            vmem((2, 8, TY), F32),
            vmem((2, 256, 128), F32),
            vmem((3, 768, TY), BF16),
            vmem((192, 2048), BF16),
            vmem((128, CP), F32),
            vmem((128, CP), BF16),
            vmem((128, 256), F32),
            sem((8,)), sem((2,)), sem((2,)), sem((2,)), sem((2,)),
            sem((12,)), sem((12,)), sem((2,)), sem((2,)), sem((2,)), sem((2,)),
        ],
        compiler_params=pltpu.CompilerParams(
            collective_id=0, has_side_effects=True, vmem_limit_bytes=63 * 1024 * 1024
        ),
    )(
        moving_image, moving_grad, fixed_grad, voxel_weight, coefficients.reshape(3, 1, CP), weight_table,
        ctrl_slot.reshape(ROWS, 8).T, weight_slot.reshape(ROWS, 8).T,
    )
    hbm = pl.BlockSpec(memory_space=pltpu.HBM)
    new, warped, energies = pl.pallas_call(
        hand_over,
        out_shape=(
            jax.ShapeDtypeStruct((3, 1, CP), F32),
            jax.ShapeDtypeStruct((TZ, TX, TY), F32),
            jax.ShapeDtypeStruct((2,), F32),
        ),
        in_specs=[whole, whole, pl.BlockSpec(memory_space=pltpu.SMEM)],
        out_specs=(hbm, hbm, hbm),
        scratch_shapes=[sem((3,))],
    )(new, warped, energies)
    return new.reshape(1, 1, 1, 3, CP), warped, energies


def solution(mesh):
    in_specs = (
        P("gz", "gx", "gy"),
        P(None, "gz", "gx", "gy"),
        P(None, "gz", "gx", "gy"),
        P("gz", "gx", "gy"),
        P("gz", "gx", "gy", None, None),
        P(),
        P("gz", "gx", "gy", None, None),
        P("gz", "gx", "gy", None, None),
    )
    out_specs = (P("gz", "gx", "gy", None, None), P("gz", "gx", "gy"), P())
    return jax.shard_map(on_device, mesh=mesh, in_specs=in_specs, out_specs=out_specs, check_vma=False)
```
